256 devices in a mesh: section: 16 (over x, y), tile: 16 (over z, core).
Axes of the slice: x: 4, y: 4, z: 8, core: 2. Of those that a mesh axis runs over, the one named last changes fastest.
Arguments:
- checkpoint: float32 [16, 128, 32768], P('section', None, 'tile'), may hold values from -5 to 5
- prior_llr: float32 [32768], P('tile'), may hold values from 0.5 to 3
- retention: float32 [32768], P('tile'), may hold values from 0 to 1
- syndrome: int32 [128, 32768], P(None, 'tile'), may hold values 0 or 1
- labels: int32 [128, 32768], P(None, 'tile'), may hold values 0 or 1
- tile_cols: int32 [768], P('tile'), may hold values from 0 to 17, as said below
- tile_count: int32 [16], P('tile'), may hold values from 24 to 48, as said below
- pattern: int32 [768, 128, 128], P('tile'), may hold values 0 or 1
- gate_weight: float32 [768], P('tile'), may hold values from 0.1 to 0.4
- msg_weight: float32 [768], P('tile'), may hold values from 0.5 to 1.5
Outputs:
- input_grads: float32 [16, 128, 32768], P('section', None, 'tile')
- gate_grads: float32 [768], P('tile')
- msg_grads: float32 [768], P('tile')
- prior_grads: float32 [32768], P('tile')
The draws below stay inside these ranges and needn't reach their ends.
Inputs may be any that keep to these rules, and one draw needn't show every extreme that they name: `tile_cols`: entries name a block of the shard's extended variable range: 0 is the last block of the shard before, 17 the first block of the shard after. Live slots of a shard are its first tile_count slots.
All inputs are finite; a program needn't handle non-finite values. No bound on the sum of `syndrome` or of `labels` or of `pattern` on one device may be relied on, other than what follows from the above.
Results may differ from the reference program's by a relative error of at most 0.0075.
Values may be sent and summed in bfloat16 or wider, within the bound.
No kernel may reach another device: no remote copies, remote signals or barrier semaphores. Data moves between devices by JAX's collectives and lax.ppermute only.
A program may use at most 64 MiB of HBM per device.

```python
import math
import jax
import jax.numpy as jnp

BLK = 128
CB_DEV = 16
VB_DEV = 16
TPC = 3
ITER_SEC = 1
SECTIONS = 16
SHOTS = 128
TILES_DEV = 48
NTILES = 768
NV = 32768
NC = 32768


def draw_tile_cols(key, part):
    shards = NTILES // TILES_DEV
    slot_index = jnp.arange(TILES_DEV, dtype=jnp.int32)
    centre = slot_index % CB_DEV * VB_DEV // CB_DEV + 1
    offsets = jax.random.randint(key, (shards, TILES_DEV), -1, 2, dtype=jnp.int32)
    columns = jnp.clip(centre[None, :] + offsets, 0, VB_DEV + 1)
    columns = columns.at[:, 0].set(0)
    columns = columns.at[:, CB_DEV - 1].set(VB_DEV + 1)
    return columns.reshape(NTILES).astype(jnp.int32)


def draw_tile_count(key, part):
    shards = NTILES // TILES_DEV
    key_counts, key_full, key_light = jax.random.split(key, 3)
    counts = jax.random.randint(key_counts, (shards,), TILES_DEV // 2, TILES_DEV + 1, dtype=jnp.int32)
    full_shard = jax.random.randint(key_full, (), 0, shards, dtype=jnp.int32)
    light_shard = (full_shard + 1 + jax.random.randint(key_light, (), 0, shards - 1, dtype=jnp.int32)) % shards
    counts = counts.at[full_shard].set(TILES_DEV)
    counts = counts.at[light_shard].set(TILES_DEV // 2)
    return counts.astype(jnp.int32)


def draw_retention(key, part):
    spread = jax.random.uniform(key, (NV,), jnp.float32)
    low_end = 0.2
    high_end = 25.0
    decay_rate = jnp.exp(jnp.log(low_end) + spread * (jnp.log(high_end) - jnp.log(low_end)))
    return jnp.exp(-decay_rate / (SECTIONS * ITER_SEC)).astype(jnp.float32)


def plant(result, key, low, top_value):
    place = [jax.random.randint(jax.random.fold_in(key, axis), (), 0, length) for axis, length in enumerate(result.shape)]
    widest = result.shape.index(max(result.shape))
    beside = place[:widest] + [(place[widest] + 1) % result.shape[widest]] + place[widest + 1:]
    return result.at[tuple(place)].set(low).at[tuple(beside)].set(top_value)


def steps_of(stream_key, shape, cuts, low, high):
    level = 1.0
    for axis_at, shards_of in cuts:
        draws = jax.random.uniform(jax.random.fold_in(jax.random.fold_in(stream_key, 6), axis_at), (shards_of,), jnp.float32, low / len(cuts), high / len(cuts))
        level = level * jnp.repeat(jnp.exp(draws), shape[axis_at] // shards_of).reshape((-1,) + (1,) * (len(shape) - 1 - axis_at))
    return level


def scatter_about(key, dims, scale, bound, cuts=(), kind=jnp.bfloat16):
    drawn = scale * jax.random.normal(key, dims, jnp.float32)
    if cuts:
        drawn = drawn * steps_of(key, dims, cuts, -0.22, 0.18)
    return jnp.clip(drawn, -bound, bound).astype(kind)


def setup_inputs(seed: int = 0) -> dict:
    key_of = jax.random.split(jax.random.key(seed), 11)
    return {
        "checkpoint": scatter_about(key_of[0], (SECTIONS, SHOTS, NV), 1.0, 5.0, ((0, 16), (2, 16)), jnp.float32),
        "prior_llr": jnp.clip(jnp.exp(math.log(3.0) - 1.7917595 * jax.random.uniform(key_of[1], (NV,), jnp.float32) ** steps_of(key_of[1], (NV,), ((0, 16),), -0.2, 0.2)), 0.5, 3.0),
        "retention": draw_retention(jax.random.fold_in(key_of[10], 71), 0),
        "syndrome": plant((jax.random.randint(key_of[3], (SHOTS, NC), 0, 8) < 1).astype(jnp.int32), jax.random.fold_in(key_of[3], 1), 0, 1),
        "labels": plant((jax.random.randint(key_of[4], (SHOTS, NV), 0, 16) < 1).astype(jnp.int32), jax.random.fold_in(key_of[4], 1), 0, 1),
        "tile_cols": draw_tile_cols(jax.random.fold_in(key_of[10], 71), 0),
        "tile_count": draw_tile_count(jax.random.fold_in(key_of[10], 71), 0),
        "pattern": plant((jax.random.randint(key_of[7], (NTILES, BLK, BLK), 0, BLK) < 2).astype(jnp.int32), jax.random.fold_in(key_of[7], 1), 0, 1),
        "gate_weight": jnp.clip(0.1 + 0.3 * jax.random.uniform(key_of[8], (NTILES,), jnp.float32) ** steps_of(key_of[8], (NTILES,), ((0, 16),), -0.2, 0.2), 0.1, 0.4),
        "msg_weight": jnp.clip(0.5 + 1.0 * jax.random.uniform(key_of[9], (NTILES,), jnp.float32) ** steps_of(key_of[9], (NTILES,), ((0, 16),), -0.2, 0.2), 0.5, 1.5),
    }


def pick_blocks(field_rows, block_index):
    rows_count = field_rows.shape[0]
    padded = jnp.pad(field_rows, ((0, 0), (BLK, BLK)))
    return jnp.take(padded.reshape(rows_count, -1, BLK), block_index, axis=1)


def spread_blocks(per_tile, block_index):
    rows_count = per_tile.shape[0]
    placed = jax.ops.segment_sum(jnp.transpose(per_tile, (1, 0, 2)), block_index, num_segments=NV // BLK + 2)
    whole_rows = jnp.transpose(placed, (1, 0, 2)).reshape(rows_count, -1)
    return whole_rows[:, BLK:-BLK]


def sum_rows(per_tile):
    rows_count = per_tile.shape[0]
    shaped = per_tile.reshape(rows_count, NTILES // TILES_DEV, TPC, CB_DEV, BLK)
    return jnp.sum(shaped, axis=2).reshape(rows_count, -1)


def repeat_rows(check_rows):
    rows_count = check_rows.shape[0]
    shaped = check_rows.reshape(rows_count, NTILES // TILES_DEV, 1, CB_DEV, BLK)
    shaped = jnp.broadcast_to(shaped, (rows_count, NTILES // TILES_DEV, TPC, CB_DEV, BLK))
    return shaped.reshape(rows_count, NTILES, BLK)


def reference(checkpoint, prior_llr, retention, syndrome, labels, tile_cols, tile_count, pattern, gate_weight, msg_weight):
    tile_index = jnp.arange(NTILES, dtype=jnp.int32)
    owner_shard = (tile_index // TILES_DEV).astype(jnp.int32)
    live_tiles = ((tile_index % TILES_DEV) < tile_count[owner_shard]).astype(jnp.float32)
    block_index = (owner_shard * VB_DEV + tile_cols).astype(jnp.int32)
    matrix = pattern.astype(jnp.float32)
    gate_scale = gate_weight * live_tiles
    msg_scale = msg_weight * live_tiles
    check_signs = 1.0 - 2.0 * syndrome.astype(jnp.float32)
    gate_acc = jnp.zeros((NTILES,), jnp.float32)
    msg_acc = jnp.zeros((NTILES,), jnp.float32)
    prior_acc = jnp.zeros((NV,), jnp.float32)
    carried = jnp.zeros((SHOTS, NV), jnp.float32)
    collected = []
    for section_index in reversed(range(SECTIONS)):
        marginal = checkpoint[section_index]
        saved_states = []
        for level_index in range(ITER_SEC):
            softened = jnp.tanh(0.5 * marginal).astype(jnp.bfloat16)
            chosen = pick_blocks(softened, block_index).astype(jnp.float32)
            to_checks = jnp.einsum("stc,trc->str", chosen, matrix)
            check_tanh = jnp.tanh(sum_rows(to_checks * gate_scale[None, :, None]))
            check_out = (check_signs * check_tanh).astype(jnp.bfloat16)
            to_vars = jnp.einsum("str,trc->stc", repeat_rows(check_out).astype(jnp.float32), matrix)
            message_sum = spread_blocks(to_vars * msg_scale[None, :, None], block_index)
            saved_states.append((marginal, check_tanh, to_checks, to_vars))
            marginal = retention * marginal + (1.0 - retention) * (prior_llr + message_sum)
        if section_index == SECTIONS - 1:
            target = labels.astype(jnp.float32)
            grad_now = target * jax.nn.sigmoid(marginal) - (1.0 - target) * jax.nn.sigmoid(-marginal)
        else:
            grad_now = carried
        for level_index in reversed(range(ITER_SEC)):
            marginal, check_tanh, to_checks, to_vars = saved_states[level_index]
            fresh_grad = (1.0 - retention) * grad_now
            prior_acc = prior_acc + jnp.sum(fresh_grad, axis=0)
            picked = pick_blocks(fresh_grad.astype(jnp.bfloat16), block_index).astype(jnp.float32)
            msg_acc = msg_acc + live_tiles * jnp.sum(picked * to_vars, axis=(0, 2))
            back_checks = jnp.einsum("stc,trc->str", picked, matrix)
            upward = sum_rows(back_checks * msg_scale[None, :, None])
            slope_rows = (upward * check_signs * (1.0 - check_tanh * check_tanh)).astype(jnp.bfloat16)
            slope_tiles = repeat_rows(slope_rows).astype(jnp.float32)
            gate_acc = gate_acc + live_tiles * jnp.sum(slope_tiles * to_checks, axis=(0, 2))
            back_vars = jnp.einsum("str,trc->stc", slope_tiles, matrix)
            downward = spread_blocks(back_vars * gate_scale[None, :, None], block_index)
            softened = jnp.tanh(0.5 * marginal)
            grad_now = retention * grad_now + 0.5 * downward * (1.0 - softened * softened)
        carried = grad_now
        collected.append(grad_now)
    input_grads = jnp.stack(collected[::-1], axis=0)
    return (input_grads, gate_acc, msg_acc, prior_acc)
```

```python
import functools

import jax
import jax.numpy as jnp
from jax import lax
from jax.experimental import pallas as pl
from jax.experimental.pallas import tpu as pltpu
from jax.sharding import PartitionSpec as P

BLK = 128
NB = 16
EXT = NB + 2
TPC = 3
TILES = NB * TPC
SEC = 16
SH = 8
GRAD_LANES = 640
LANES = NB * BLK
VMEM_LIMIT = 16 * 1024 * 1024
F32 = jnp.float32
BF16 = jnp.bfloat16
VSPEC = pl.BlockSpec(memory_space=pltpu.VMEM)
SSPEC = pl.BlockSpec(memory_space=pltpu.SMEM)

CORE_PAIRS = [(i, i ^ 1) for i in range(16)]
Z_PAIRS = [(i, (i + 1) % 16 if i % 2 else (i - 1) % 16) for i in range(16)]


def nt(a, b):
    return lax.dot_general(a, b, (((1,), (1,)), ((), ())), preferred_element_type=F32)


def nn(a, b):
    return lax.dot_general(a, b, (((1,), (0,)), ((), ())), preferred_element_type=F32)


def call(body, outs, args, n_smem, scratch=(), flops=0, bytes_accessed=0):
    return pl.pallas_call(
        body,
        out_shape=outs,
        in_specs=[SSPEC] * n_smem + [VSPEC] * (len(args) - n_smem),
        out_specs=[VSPEC] * len(outs),
        scratch_shapes=list(scratch),
        compiler_params=pltpu.CompilerParams(vmem_limit_bytes=VMEM_LIMIT),
        cost_estimate=pl.CostEstimate(flops=flops, bytes_accessed=bytes_accessed, transcendentals=0),
    )(*args)


def send_edges(acc_ref, ints, sendc, sendz):
    sendc[0] = acc_ref[NB]
    sendc[1] = acc_ref[ints[TILES]]
    sendz[0] = acc_ref[NB + 1]
    sendz[1] = acc_ref[ints[TILES + 1]]


def received(acc_ref, block, recvc, recvz, floats):
    own = acc_ref[block]
    even = floats[2 * TILES]
    zmask = floats[2 * TILES + 1]
    if block == 0:
        return own + (recvz[0] * (zmask * even) + recvc[0] * (1.0 - even))
    if block == NB - 1:
        return own + (recvz[0] * (zmask * (1.0 - even)) + recvc[0] * even)
    if block == NB:
        return own + recvc[1]
    if block == NB + 1:
        return (own + recvz[1]) * zmask
    return own


def forward_body(ints, floats, marg, pattern, signs, th_out, u_out, gv_out, sendc, sendz, tb):
    zmask = floats[2 * TILES + 1]
    for block in range(EXT):
        th = jnp.tanh(0.5 * marg[:, block * BLK : (block + 1) * BLK])
        if block == NB + 1:
            th = th * zmask
        th_out[block] = th
        tb[block] = th.astype(BF16)
    gv_out[...] = jnp.zeros_like(gv_out)
    for row in range(NB):
        total = None
        for slot in range(TPC):
            tile = slot * NB + row
            part = nt(tb[ints[tile]], pattern[tile]) * floats[tile]
            total = part if total is None else total + part
        sign = signs[:, row * BLK : (row + 1) * BLK]
        soft = jnp.tanh(total).reshape(SEC, SH, BLK) * sign[None]
        u_out[row] = soft.reshape(SEC * SH, BLK)
    for row in range(NB):
        last = u_out[row, (SEC - 1) * SH :, :].astype(BF16)
        for slot in range(TPC):
            tile = slot * NB + row
            gv_out[ints[tile]] += nn(last, pattern[tile]) * floats[TILES + tile]
    send_edges(gv_out, ints, sendc, sendz)


def backward_rows(ints, floats, section, u_ref, signs, pattern, qs, dz_out, acc_out):
    acc_out[...] = jnp.zeros_like(acc_out)
    for row in range(NB):
        total = None
        for slot in range(TPC):
            tile = slot * NB + row
            part = nt(qs[ints[tile]].astype(BF16), pattern[tile]) * floats[TILES + tile]
            total = part if total is None else total + part
        u = u_ref[row, section * SH : (section + 1) * SH, :]
        sign = signs[:, row * BLK : (row + 1) * BLK]
        dz_out[row] = (total * sign * (1.0 - u * u)).astype(BF16).astype(F32)
    for row in range(NB):
        dz = dz_out[row].astype(BF16)
        for slot in range(TPC):
            tile = slot * NB + row
            acc_out[ints[tile]] += nn(dz, pattern[tile]) * floats[tile]


def first_body(ints, floats, marg, gv, recvc, recvz, ret, prior, labels, u_ref, signs, pattern,
               g_out, q_out, dz_out, acc_out, sendc, sendz):
    zmask = floats[2 * TILES + 1]
    for block in range(EXT):
        lanes = slice(block * BLK, (block + 1) * BLK)
        r = ret[0:1, lanes]
        message = received(gv, block, recvc, recvz, floats)
        level = marg[(SEC - 1) * SH :, lanes]
        f = r * level + (1.0 - r) * (prior[0:1, lanes] + message)
        y = labels[:, lanes]
        g = y * jax.nn.sigmoid(f) - (1.0 - y) * jax.nn.sigmoid(-f)
        if block == NB + 1:
            g = g * zmask
        g_out[block] = g
        q_out[block] = ((1.0 - r) * g).astype(BF16).astype(F32)
    backward_rows(ints, floats, SEC - 1, u_ref, signs, pattern, q_out, dz_out, acc_out)
    send_edges(acc_out, ints, sendc, sendz)


def next_gradient(section, g_in, acc_in, recvc, recvz, th_ref, ret, floats, block):
    r = ret[0:1, block * BLK : (block + 1) * BLK]
    th = th_ref[block, section * SH : (section + 1) * SH, :]
    down = received(acc_in, block, recvc, recvz, floats)
    return r * g_in[block] + 0.5 * down * (1.0 - th * th)


def step_body(section, ints, floats, g_in, acc_in, recvc, recvz, ret, th_ref, u_ref, signs, pattern,
              g_out, q_out, dz_out, acc_out, sendc, sendz):
    for block in range(EXT):
        g = next_gradient(section + 1, g_in, acc_in, recvc, recvz, th_ref, ret, floats, block)
        g_out[block] = g
        r = ret[0:1, block * BLK : (block + 1) * BLK]
        q_out[block] = ((1.0 - r) * g).astype(BF16).astype(F32)
    backward_rows(ints, floats, section, u_ref, signs, pattern, q_out, dz_out, acc_out)
    send_edges(acc_out, ints, sendc, sendz)


def weights_body(section_high, count, ints, *refs):
    th_ref, u_ref, pattern, gate_in, msg_in = refs[:5]
    q_refs = refs[5 : 5 + count]
    dz_refs = refs[5 + count : 5 + 2 * count]
    gate_out, msg_out = refs[5 + 2 * count :]
    first = (section_high - count + 1) * SH
    rows = slice(first, first + count * SH)
    for row in range(NB):
        dz = jnp.concatenate([ref[row] for ref in dz_refs], axis=0).astype(BF16)
        u = u_ref[row, rows, :].astype(BF16).astype(F32)
        for slot in range(TPC):
            tile = slot * NB + row
            column = ints[tile]
            t = th_ref[column, rows, :].astype(BF16).astype(F32)
            gate = nn(dz, pattern[tile]) * t
            gate_out[tile] = gate_in[tile] + jnp.sum(gate.reshape(count, SH, BLK), axis=0)
            q = jnp.concatenate([ref[column] for ref in q_refs], axis=0).astype(BF16)
            msg = nt(q, pattern[tile]) * u
            msg_out[tile] = msg_in[tile] + jnp.sum(msg.reshape(count, SH, BLK), axis=0)


def split(value):
    high = value.astype(BF16).astype(F32)
    return high, value - high


def pack_body(floats, acc_in, recvc, recvz, ret, th_ref, gate, msg, *refs):
    g_refs = refs[:SEC]
    out = refs[SEC]
    for block in range(NB):
        lanes = slice(block * BLK, (block + 1) * BLK)
        entering = [next_gradient(0, g_refs[0], acc_in, recvc, recvz, th_ref, ret, floats, block)]
        entering += [g_refs[section][block] for section in range(SEC - 1)]
        for pair in range(SEC // 2):
            both = jnp.concatenate(entering[2 * pair : 2 * pair + 2], axis=0)
            out[pair * 2 * SH : (pair + 1) * 2 * SH, lanes] = both.astype(BF16)
    priors = []
    for block in range(NB):
        total = g_refs[0][block]
        for section in range(1, SEC):
            total = total + g_refs[section][block]
        r = ret[0:1, block * BLK : (block + 1) * BLK]
        priors.append((1.0 - r) * jnp.sum(total, axis=0, keepdims=True))
    prior_high, prior_low = [], []
    for half in range(2):
        high, low = split(jnp.concatenate(priors[half * SH : (half + 1) * SH], axis=0))
        prior_high.append(high)
        prior_low.append(low)
    gate_rows = jnp.sum(gate[...], axis=1)
    msg_rows = jnp.sum(msg[...], axis=1)
    gate_sum = jnp.sum(gate_rows, axis=1, keepdims=True)
    msg_sum = jnp.sum(msg_rows, axis=1, keepdims=True)
    tile_index = lax.broadcasted_iota(jnp.int32, (TILES, BLK), 0)
    lane_index = lax.broadcasted_iota(jnp.int32, (TILES, BLK), 1)
    merged = jnp.where(tile_index == lane_index, gate_sum, 0.0) + jnp.where(
        tile_index + TILES == lane_index, msg_sum, 0.0
    )
    high, low = split(jnp.sum(merged, axis=0, keepdims=True))
    weights = jnp.concatenate([high, low, jnp.zeros((SH - 2, BLK), F32)], axis=0)
    for index, value in enumerate(prior_high + prior_low + [weights]):
        doubled = jnp.concatenate([value, value], axis=0).astype(BF16)
        lanes = slice(LANES + index * BLK, LANES + (index + 1) * BLK)
        for pair in range(SEC // 2):
            out[pair * 2 * SH : (pair + 1) * 2 * SH, lanes] = doubled


def on_device(
    checkpoint,
    prior_llr,
    retention,
    syndrome,
    labels,
    tile_cols,
    tile_count,
    pattern,
    gate_weight,
    msg_weight,
):
    shard = lax.axis_index("tile")
    group = lax.axis_index("section")
    even = shard % 2 == 0
    has_z = jnp.logical_and(shard != 0, shard != SEC - 1)

    def own_edges(x):
        first, last = x[..., :BLK], x[..., -BLK:]
        return jnp.where(even, last, first), jnp.where(even, first, last)

    def exchange(core, z):
        return lax.ppermute(core, "tile", CORE_PAIRS), lax.ppermute(z, "tile", Z_PAIRS)

    levels = checkpoint[0]
    my_labels = lax.dynamic_slice_in_dim(labels, group * SH, SH, 0).astype(F32)
    my_signs = 1.0 - 2.0 * lax.dynamic_slice_in_dim(syndrome, group * SH, SH, 0).astype(F32)
    fixed = jnp.concatenate(
        [prior_llr[None], retention[None], jnp.zeros((SH - 2, LANES), F32)], axis=0
    )
    together = jnp.concatenate([levels, my_labels, fixed], axis=0)
    halo_core, halo_z = exchange(*own_edges(together))

    slots = jnp.arange(TILES, dtype=jnp.int32)
    live = (slots < tile_count[0]).astype(F32)
    low_slot = jnp.where(even, NB + 1, NB)
    high_slot = jnp.where(even, NB, NB + 1)
    columns = jnp.where(
        tile_cols == 0, low_slot, jnp.where(tile_cols == NB + 1, high_slot, tile_cols - 1)
    )
    core_side = jnp.where(even, NB - 1, 0)
    z_side = jnp.where(even, 0, NB - 1)
    ints = jnp.concatenate([columns, core_side[None], z_side[None]]).astype(jnp.int32)
    floats = jnp.concatenate(
        [gate_weight * live, msg_weight * live, jnp.stack([even, has_z]).astype(F32)]
    )
    patterns = pattern.astype(BF16)

    wide = jnp.concatenate([together, halo_core, halo_z], axis=1)
    labels_ext = wide[SEC * SH : SEC * SH + SH]
    prior_ext = wide[SEC * SH + SH : SEC * SH + SH + 1]
    ret_ext = wide[SEC * SH + SH + 1 : SEC * SH + SH + 2]
    sent = wide[: SEC * SH].astype(jnp.float16).reshape(SEC, SH, EXT * BLK)
    marg = lax.all_to_all(sent, "section", 0, 0, tiled=True)
    marg = marg.reshape(SEC * SH, EXT * BLK).astype(F32)

    def shape(*dims, dtype=F32):
        return jax.ShapeDtypeStruct(dims, dtype)

    edge = shape(2, SH, BLK)
    field = shape(EXT, SH, BLK)
    rows = shape(NB, SH, BLK)
    th, u, gv, core, z = call(
        forward_body,
        [shape(EXT, SEC * SH, BLK), shape(NB, SEC * SH, BLK), field, edge, edge],
        [ints, floats, marg, patterns, my_signs],
        2,
        scratch=[pltpu.VMEM((EXT, SEC * SH, BLK), BF16)],
    )
    core, z = exchange(core, z)
    g, q, dz, acc, core, z = call(
        first_body,
        [field, field, rows, field, edge, edge],
        [ints, floats, marg, gv, core, z, ret_ext, prior_ext, labels_ext, u, my_signs, patterns],
        2,
    )
    leaving = {SEC - 1: g}
    saved = [(q, dz)]
    gate = jnp.zeros((TILES, SH, BLK), F32)
    msg = jnp.zeros((TILES, SH, BLK), F32)
    group_size = 4
    for section in reversed(range(SEC - 1)):
        core, z = exchange(core, z)
        g, q, dz, acc, core, z = call(
            functools.partial(step_body, section),
            [field, field, rows, field, edge, edge],
            [ints, floats, g, acc, core, z, ret_ext, th, u, my_signs, patterns],
            2,
        )
        leaving[section] = g
        saved.append((q, dz))
        if len(saved) == group_size:
            saved = saved[::-1]
            gate, msg = call(
                functools.partial(weights_body, section + group_size - 1, group_size),
                [shape(TILES, SH, BLK)] * 2,
                [ints, th, u, patterns, gate, msg] + [s[0] for s in saved] + [s[1] for s in saved],
                1,
            )
            saved = []
    core, z = exchange(core, z)
    (packed,) = call(
        pack_body,
        [shape(SEC * SH, LANES + GRAD_LANES, dtype=BF16)],
        [floats, acc, core, z, ret_ext, th, gate, msg] + [leaving[s] for s in range(SEC)],
        1,
    )
    got = lax.all_to_all(packed.reshape(SEC, SH, LANES + GRAD_LANES), "section", 0, 0, tiled=True)
    grads = jnp.sum(got[:, :, LANES:].astype(F32), axis=0)
    prior = (grads[:, : 2 * BLK] + grads[:, 2 * BLK : 4 * BLK]).reshape(SH, 2, BLK)
    prior = prior.transpose(1, 0, 2).reshape(LANES)
    weights = grads[0, 4 * BLK :] + grads[1, 4 * BLK :]
    input_grads = got[:, :, :LANES].astype(F32).reshape(1, SEC * SH, LANES)
    return input_grads, weights[:TILES] * live, weights[TILES : 2 * TILES] * live, prior


def solution(mesh):
    placed = (
        P("section", None, "tile"),
        P("tile"),
        P("tile"),
        P(None, "tile"),
        P(None, "tile"),
        P("tile"),
        P("tile"),
        P("tile", None, None),
        P("tile"),
        P("tile"),
    )
    return jax.shard_map(
        on_device,
        mesh=mesh,
        in_specs=placed,
        out_specs=(P("section", None, "tile"), P("tile"), P("tile"), P("tile")),
        check_vma=False,
    )
```

```python
import functools

import jax
import jax.numpy as jnp
from jax import lax
from jax.experimental import pallas as pl
from jax.experimental.pallas import tpu as pltpu
from jax.sharding import PartitionSpec as P

BLK = 128
NB = 16
EXT = NB + 2
TPC = 3
TILES = NB * TPC
SEC = 16
SH = 8
GRAD_LANES = 640
LANES = NB * BLK
VMEM_LIMIT = 8 * 1024 * 1024
PREP_ROWS = 4
F32 = jnp.float32
BF16 = jnp.bfloat16
VSPEC = pl.BlockSpec(memory_space=pltpu.VMEM)
SSPEC = pl.BlockSpec(memory_space=pltpu.SMEM)

CORE_PAIRS = [(i, i ^ 1) for i in range(16)]
Z_PAIRS = [(i, (i + 1) % 16 if i % 2 else (i - 1) % 16) for i in range(16)]


def nn(a, b):
    return lax.dot_general(a, b, (((1,), (0,)), ((), ())), preferred_element_type=F32)


def call(body, outs, args, n_smem, scratch=(), flops=0, bytes_accessed=0):
    return pl.pallas_call(
        body,
        out_shape=outs,
        in_specs=[SSPEC] * n_smem + [VSPEC] * (len(args) - n_smem),
        out_specs=[VSPEC] * len(outs),
        scratch_shapes=list(scratch),
        compiler_params=pltpu.CompilerParams(vmem_limit_bytes=VMEM_LIMIT),
        cost_estimate=pl.CostEstimate(flops=flops, bytes_accessed=bytes_accessed, transcendentals=0),
    )(*args)


def send_edges(acc_ref, ints, sendc, sendz):
    sendc[0] = acc_ref[NB]
    sendc[1] = acc_ref[ints[TILES]]
    sendz[0] = acc_ref[NB + 1]
    sendz[1] = acc_ref[ints[TILES + 1]]


def received(acc_ref, block, recvc, recvz, floats):
    own = acc_ref[block]
    even = floats[2 * TILES]
    zmask = floats[2 * TILES + 1]
    if block == 0:
        return own + (recvz[0] * (zmask * even) + recvc[0] * (1.0 - even))
    if block == NB - 1:
        return own + (recvz[0] * (zmask * (1.0 - even)) + recvc[0] * even)
    if block == NB:
        return own + recvc[1]
    if block == NB + 1:
        return (own + recvz[1]) * zmask
    return own


def forward_body(ints, floats, marg, by_check, by_var, signs, th_out, u_out, gv_out, sendc, sendz, tb):
    zmask = floats[2 * TILES + 1]
    for block in range(EXT):
        th = jnp.tanh(0.5 * marg[:, block * BLK : (block + 1) * BLK])
        if block == NB + 1:
            th = th * zmask
        th_out[block] = th
        tb[block] = th.astype(BF16)
    gv_out[...] = jnp.zeros_like(gv_out)
    for row in range(NB):
        total = None
        for slot in range(TPC):
            tile = slot * NB + row
            part = nn(tb[ints[tile]], by_var[row, slot * BLK : (slot + 1) * BLK, :]) * floats[tile]
            total = part if total is None else total + part
        sign = signs[:, row * BLK : (row + 1) * BLK]
        soft = jnp.tanh(total).reshape(SEC, SH, BLK) * sign[None]
        u_out[row] = soft.reshape(SEC * SH, BLK)
    for row in range(NB):
        parts = nn(u_out[row, (SEC - 1) * SH :, :].astype(BF16), by_check[row])
        for slot in range(TPC):
            tile = slot * NB + row
            gv_out[ints[tile]] += parts[:, slot * BLK : (slot + 1) * BLK] * floats[TILES + tile]
    send_edges(gv_out, ints, sendc, sendz)


def backward_rows(ints, floats, section, u_ref, signs, by_check, by_var, qs, dz_out, acc_out):
    acc_out[...] = jnp.zeros_like(acc_out)
    for row in range(NB):
        tiles = [slot * NB + row for slot in range(TPC)]
        scaled = [(qs[ints[tile]] * floats[TILES + tile]).astype(BF16) for tile in tiles]
        total = nn(jnp.concatenate(scaled, axis=1), by_var[row])
        u = u_ref[row, section * SH : (section + 1) * SH, :]
        sign = signs[:, row * BLK : (row + 1) * BLK]
        dz_out[row] = (total * sign * (1.0 - u * u)).astype(BF16).astype(F32)
    for row in range(NB):
        parts = nn(dz_out[row].astype(BF16), by_check[row])
        for slot in range(TPC):
            tile = slot * NB + row
            acc_out[ints[tile]] += parts[:, slot * BLK : (slot + 1) * BLK] * floats[tile]


def first_body(ints, floats, marg, gv, recvc, recvz, ret, prior, labels, u_ref, signs, by_check,
               by_var, g_out, q_out, dz_out, acc_out, sendc, sendz):
    zmask = floats[2 * TILES + 1]
    for block in range(EXT):
        lanes = slice(block * BLK, (block + 1) * BLK)
        r = ret[0:1, lanes]
        message = received(gv, block, recvc, recvz, floats)
        level = marg[(SEC - 1) * SH :, lanes]
        f = r * level + (1.0 - r) * (prior[0:1, lanes] + message)
        y = labels[:, lanes]
        g = y * jax.nn.sigmoid(f) - (1.0 - y) * jax.nn.sigmoid(-f)
        if block == NB + 1:
            g = g * zmask
        g_out[block] = g
        q_out[block] = (1.0 - r) * g
    backward_rows(ints, floats, SEC - 1, u_ref, signs, by_check, by_var, q_out, dz_out, acc_out)
    send_edges(acc_out, ints, sendc, sendz)


def next_gradient(section, g_in, acc_in, recvc, recvz, th_ref, ret, floats, block):
    r = ret[0:1, block * BLK : (block + 1) * BLK]
    th = th_ref[block, section * SH : (section + 1) * SH, :]
    down = received(acc_in, block, recvc, recvz, floats)
    return r * g_in[block] + 0.5 * down * (1.0 - th * th)


def step_body(section, ints, floats, g_in, acc_in, recvc, recvz, ret, th_ref, u_ref, signs, by_check,
              by_var, g_out, q_out, dz_out, acc_out, sendc, sendz):
    for block in range(EXT):
        g = next_gradient(section + 1, g_in, acc_in, recvc, recvz, th_ref, ret, floats, block)
        g_out[block] = g
        r = ret[0:1, block * BLK : (block + 1) * BLK]
        q_out[block] = (1.0 - r) * g
    backward_rows(ints, floats, section, u_ref, signs, by_check, by_var, q_out, dz_out, acc_out)
    send_edges(acc_out, ints, sendc, sendz)


def weights_body(section_high, count, ints, *refs):
    th_ref, u_ref, by_check, gate_in, msg_in = refs[:5]
    q_refs = refs[5 : 5 + count]
    dz_refs = refs[5 + count : 5 + 2 * count]
    gate_out, msg_out = refs[5 + 2 * count :]
    first = (section_high - count + 1) * SH
    rows = slice(first, first + count * SH)
    for row in range(NB):
        dz = jnp.concatenate([ref[row] for ref in dz_refs], axis=0).astype(BF16)
        gates = nn(dz, by_check[row])
        msgs = nn(u_ref[row, rows, :].astype(BF16), by_check[row])
        for slot in range(TPC):
            tile = slot * NB + row
            lanes = slice(slot * BLK, (slot + 1) * BLK)
            column = ints[tile]
            gate = gates[:, lanes] * th_ref[column, rows, :].astype(BF16).astype(F32)
            gate_out[tile] = gate_in[tile] + jnp.sum(gate.reshape(count, SH, BLK), axis=0)
            q = jnp.concatenate([ref[column] for ref in q_refs], axis=0).astype(BF16).astype(F32)
            msg = msgs[:, lanes] * q
            msg_out[tile] = msg_in[tile] + jnp.sum(msg.reshape(count, SH, BLK), axis=0)


def prepare_body(pattern, by_check, by_var):
    for row in range(PREP_ROWS):
        for slot in range(TPC):
            lanes = slice(slot * BLK, (slot + 1) * BLK)
            tile = pattern[slot, row].astype(F32)
            by_check[row, :, lanes] = tile.astype(BF16)
            by_var[row, lanes, :] = tile.T.astype(BF16)


def prepare(pattern):
    return pl.pallas_call(
        prepare_body,
        grid=(NB // PREP_ROWS,),
        in_specs=[pl.BlockSpec((TPC, PREP_ROWS, BLK, BLK), lambda i: (0, i, 0, 0))],
        out_specs=[
            pl.BlockSpec((PREP_ROWS, BLK, TPC * BLK), lambda i: (i, 0, 0)),
            pl.BlockSpec((PREP_ROWS, TPC * BLK, BLK), lambda i: (i, 0, 0)),
        ],
        out_shape=[
            jax.ShapeDtypeStruct((NB, BLK, TPC * BLK), BF16),
            jax.ShapeDtypeStruct((NB, TPC * BLK, BLK), BF16),
        ],
        compiler_params=pltpu.CompilerParams(vmem_limit_bytes=VMEM_LIMIT),
        cost_estimate=pl.CostEstimate(flops=10**9, bytes_accessed=6 * 2**20, transcendentals=0),
    )(pattern.reshape(TPC, NB, BLK, BLK))


def split(value):
    high = value.astype(BF16).astype(F32)
    return high, value - high


def pack_body(floats, acc_in, recvc, recvz, ret, th_ref, gate, msg, *refs):
    g_refs = refs[:SEC]
    out = refs[SEC]
    for block in range(NB):
        lanes = slice(block * BLK, (block + 1) * BLK)
        entering = [next_gradient(0, g_refs[0], acc_in, recvc, recvz, th_ref, ret, floats, block)]
        entering += [g_refs[section][block] for section in range(SEC - 1)]
        for pair in range(SEC // 2):
            both = jnp.concatenate(entering[2 * pair : 2 * pair + 2], axis=0)
            out[pair * 2 * SH : (pair + 1) * 2 * SH, lanes] = both.astype(BF16)
    priors = []
    for block in range(NB):
        total = g_refs[0][block]
        for section in range(1, SEC):
            total = total + g_refs[section][block]
        r = ret[0:1, block * BLK : (block + 1) * BLK]
        priors.append((1.0 - r) * jnp.sum(total, axis=0, keepdims=True))
    prior_high, prior_low = [], []
    for half in range(2):
        high, low = split(jnp.concatenate(priors[half * SH : (half + 1) * SH], axis=0))
        prior_high.append(high)
        prior_low.append(low)
    gate_rows = jnp.sum(gate[...], axis=1)
    msg_rows = jnp.sum(msg[...], axis=1)
    gate_sum = jnp.sum(gate_rows, axis=1, keepdims=True)
    msg_sum = jnp.sum(msg_rows, axis=1, keepdims=True)
    tile_index = lax.broadcasted_iota(jnp.int32, (TILES, BLK), 0)
    lane_index = lax.broadcasted_iota(jnp.int32, (TILES, BLK), 1)
    merged = jnp.where(tile_index == lane_index, gate_sum, 0.0) + jnp.where(
        tile_index + TILES == lane_index, msg_sum, 0.0
    )
    high, low = split(jnp.sum(merged, axis=0, keepdims=True))
    weights = jnp.concatenate([high, low, jnp.zeros((SH - 2, BLK), F32)], axis=0)
    for index, value in enumerate(prior_high + prior_low + [weights]):
        doubled = jnp.concatenate([value, value], axis=0).astype(BF16)
        lanes = slice(LANES + index * BLK, LANES + (index + 1) * BLK)
        for pair in range(SEC // 2):
            out[pair * 2 * SH : (pair + 1) * 2 * SH, lanes] = doubled


def on_device(
    checkpoint,
    prior_llr,
    retention,
    syndrome,
    labels,
    tile_cols,
    tile_count,
    pattern,
    gate_weight,
    msg_weight,
):
    shard = lax.axis_index("tile")
    group = lax.axis_index("section")
    even = shard % 2 == 0
    has_z = jnp.logical_and(shard != 0, shard != SEC - 1)

    def own_edges(x):
        first, last = x[..., :BLK], x[..., -BLK:]
        return jnp.where(even, last, first), jnp.where(even, first, last)

    def exchange(core, z):
        return lax.ppermute(core, "tile", CORE_PAIRS), lax.ppermute(z, "tile", Z_PAIRS)

    levels = checkpoint[0]
    my_labels = lax.dynamic_slice_in_dim(labels, group * SH, SH, 0).astype(F32)
    my_signs = 1.0 - 2.0 * lax.dynamic_slice_in_dim(syndrome, group * SH, SH, 0).astype(F32)
    fixed = jnp.stack([prior_llr, retention])
    edges = [own_edges(x) for x in (levels, my_labels, fixed)]
    pad = jnp.zeros((SH - 2, BLK), F32)
    halo_core, halo_z = exchange(
        jnp.concatenate([e[0] for e in edges] + [pad], axis=0),
        jnp.concatenate([e[1] for e in edges] + [pad], axis=0),
    )

    slots = jnp.arange(TILES, dtype=jnp.int32)
    live = (slots < tile_count[0]).astype(F32)
    low_slot = jnp.where(even, NB + 1, NB)
    high_slot = jnp.where(even, NB, NB + 1)
    columns = jnp.where(
        tile_cols == 0, low_slot, jnp.where(tile_cols == NB + 1, high_slot, tile_cols - 1)
    )
    core_side = jnp.where(even, NB - 1, 0)
    z_side = jnp.where(even, 0, NB - 1)
    ints = jnp.concatenate([columns, core_side[None], z_side[None]]).astype(jnp.int32)
    floats = jnp.concatenate(
        [gate_weight * live, msg_weight * live, jnp.stack([even, has_z]).astype(F32)]
    )
    shots = SEC * SH
    halo = jnp.concatenate([halo_core, halo_z], axis=1)
    labels_ext = jnp.concatenate([my_labels, halo[shots : shots + SH]], axis=1)
    fixed_ext = jnp.concatenate([fixed, halo[shots + SH : shots + SH + 2]], axis=1)
    prior_ext, ret_ext = fixed_ext[0:1], fixed_ext[1:2]
    sent = jnp.concatenate([levels, halo[:shots]], axis=1).astype(jnp.float16)
    sent = sent.reshape(SEC, SH, EXT * BLK)
    patterns = prepare(pattern)
    marg = lax.all_to_all(sent, "section", 0, 0, tiled=True)
    marg = marg.reshape(SEC * SH, EXT * BLK).astype(F32)

    def shape(*dims, dtype=F32):
        return jax.ShapeDtypeStruct(dims, dtype)

    edge = shape(2, SH, BLK)
    field = shape(EXT, SH, BLK)
    rows = shape(NB, SH, BLK)
    th, u, gv, core, z = call(
        forward_body,
        [shape(EXT, SEC * SH, BLK), shape(NB, SEC * SH, BLK), field, edge, edge],
        [ints, floats, marg, *patterns, my_signs],
        2,
        scratch=[pltpu.VMEM((EXT, SEC * SH, BLK), BF16)],
    )
    core, z = exchange(core, z)
    g, q, dz, acc, core, z = call(
        first_body,
        [field, field, rows, field, edge, edge],
        [ints, floats, marg, gv, core, z, ret_ext, prior_ext, labels_ext, u, my_signs, *patterns],
        2,
    )
    leaving = {SEC - 1: g}
    saved = [(q, dz)]
    gate = jnp.zeros((TILES, SH, BLK), F32)
    msg = jnp.zeros((TILES, SH, BLK), F32)
    group_size = 4
    for section in reversed(range(SEC - 1)):
        core, z = exchange(core, z)
        if not saved:
            core, z, gate, msg = lax.optimization_barrier((core, z, gate, msg))
        g, q, dz, acc, core, z = call(
            functools.partial(step_body, section),
            [field, field, rows, field, edge, edge],
            [ints, floats, g, acc, core, z, ret_ext, th, u, my_signs, *patterns],
            2,
        )
        leaving[section] = g
        saved.append((q, dz))
        if len(saved) == group_size:
            saved = saved[::-1]
            gate, msg = call(
                functools.partial(weights_body, section + group_size - 1, group_size),
                [shape(TILES, SH, BLK)] * 2,
                [ints, th, u, patterns[0], gate, msg] + [s[0] for s in saved] + [s[1] for s in saved],
                1,
                flops=2 * 2 * group_size * SH * TILES * BLK * BLK,
                bytes_accessed=4 * 2**20,
            )
            saved = []
    core, z = exchange(core, z)
    (packed,) = call(
        pack_body,
        [shape(SEC * SH, LANES + GRAD_LANES, dtype=BF16)],
        [floats, acc, core, z, ret_ext, th, gate, msg] + [leaving[s] for s in range(SEC)],
        1,
    )
    got = lax.all_to_all(packed.reshape(SEC, SH, LANES + GRAD_LANES), "section", 0, 0, tiled=True)
    grads = jnp.sum(got[:, :, LANES:].astype(F32), axis=0)
    prior = (grads[:, : 2 * BLK] + grads[:, 2 * BLK : 4 * BLK]).reshape(SH, 2, BLK)
    prior = prior.transpose(1, 0, 2).reshape(LANES)
    weights = grads[0, 4 * BLK :] + grads[1, 4 * BLK :]
    input_grads = got[:, :, :LANES].astype(F32).reshape(1, SEC * SH, LANES)
    return input_grads, weights[:TILES] * live, weights[TILES : 2 * TILES] * live, prior


def solution(mesh):
    placed = (
        P("section", None, "tile"),
        P("tile"),
        P("tile"),
        P(None, "tile"),
        P(None, "tile"),
        P("tile"),
        P("tile"),
        P("tile", None, None),
        P("tile"),
        P("tile"),
    )
    return jax.shard_map(
        on_device,
        mesh=mesh,
        in_specs=placed,
        out_specs=(P("section", None, "tile"), P("tile"), P("tile"), P("tile")),
        check_vma=False,
    )
```

```python
import functools

import jax
import jax.numpy as jnp
from jax import lax
from jax.experimental import pallas as pl
from jax.experimental.pallas import tpu as pltpu
from jax.sharding import PartitionSpec as P

BLK = 128
NB = 16
EXT = NB + 2
TPC = 3
TILES = NB * TPC
SEC = 16
SH = 8
GRAD_LANES = 640
LANES = NB * BLK
VMEM_LIMIT = 8 * 1024 * 1024
PREP_ROWS = 4
F32 = jnp.float32
BF16 = jnp.bfloat16
VSPEC = pl.BlockSpec(memory_space=pltpu.VMEM)
SSPEC = pl.BlockSpec(memory_space=pltpu.SMEM)

CORE_PAIRS = [(i, i ^ 1) for i in range(16)]
Z_PAIRS = [(i, (i + 1) % 16 if i % 2 else (i - 1) % 16) for i in range(16)]


def nn(a, b):
    return lax.dot_general(a, b, (((1,), (0,)), ((), ())), preferred_element_type=F32)


def call(body, outs, args, n_smem, scratch=(), flops=0, bytes_accessed=0):
    return pl.pallas_call(
        body,
        out_shape=outs,
        in_specs=[SSPEC] * n_smem + [VSPEC] * (len(args) - n_smem),
        out_specs=[VSPEC] * len(outs),
        scratch_shapes=list(scratch),
        compiler_params=pltpu.CompilerParams(vmem_limit_bytes=VMEM_LIMIT),
        cost_estimate=pl.CostEstimate(flops=flops, bytes_accessed=bytes_accessed, transcendentals=0),
    )(*args)


def send_edges(acc_ref, ints, sendc, sendz):
    sendc[0] = acc_ref[NB]
    sendc[1] = acc_ref[ints[TILES]]
    sendz[0] = acc_ref[NB + 1]
    sendz[1] = acc_ref[ints[TILES + 1]]


def received(acc_ref, block, recvc, recvz, floats):
    own = acc_ref[block]
    even = floats[2 * TILES]
    zmask = floats[2 * TILES + 1]
    if block == 0:
        return own + (recvz[0] * (zmask * even) + recvc[0] * (1.0 - even))
    if block == NB - 1:
        return own + (recvz[0] * (zmask * (1.0 - even)) + recvc[0] * even)
    if block == NB:
        return own + recvc[1]
    if block == NB + 1:
        return (own + recvz[1]) * zmask
    return own


def forward_body(ints, floats, marg, by_check, by_var, signs, labels, fixed, th_out, u_out, gv_out, sendc, sendz, tb):
    zmask = floats[2 * TILES + 1]
    for block in range(EXT):
        th = jnp.tanh(0.5 * marg[:, block * BLK : (block + 1) * BLK])
        if block == NB + 1:
            th = th * zmask
        th_out[block] = th
        tb[block] = th.astype(BF16)
    gv_out[...] = jnp.zeros_like(gv_out)
    for row in range(NB):
        total = None
        for slot in range(TPC):
            tile = slot * NB + row
            part = nn(tb[ints[tile]], by_var[row, slot * BLK : (slot + 1) * BLK, :]) * floats[tile]
            total = part if total is None else total + part
        sign = signs[:, row * BLK : (row + 1) * BLK]
        soft = jnp.tanh(total).reshape(SEC, SH, BLK) * sign[None]
        u_out[row] = soft.reshape(SEC * SH, BLK)
    for row in range(NB):
        parts = nn(u_out[row, (SEC - 1) * SH :, :].astype(BF16), by_check[row])
        for slot in range(TPC):
            tile = slot * NB + row
            gv_out[ints[tile]] += parts[:, slot * BLK : (slot + 1) * BLK] * floats[TILES + tile]
    send_edges(gv_out, ints, sendc, sendz)
    even = floats[2 * TILES]
    for source, row in ((labels[...], 2), (fixed[...], 3)):
        first, last = source[:, :BLK], source[:, -BLK:]
        sendc[row] = last * even + first * (1.0 - even)
        sendz[row] = first * even + last * (1.0 - even)


def backward_rows(ints, floats, section, u_ref, signs, by_check, by_var, qs, dz_out, acc_out):
    acc_out[...] = jnp.zeros_like(acc_out)
    for row in range(NB):
        tiles = [slot * NB + row for slot in range(TPC)]
        scaled = [(qs[ints[tile]] * floats[TILES + tile]).astype(BF16) for tile in tiles]
        total = nn(jnp.concatenate(scaled, axis=1), by_var[row])
        u = u_ref[row, section * SH : (section + 1) * SH, :]
        sign = signs[:, row * BLK : (row + 1) * BLK]
        dz_out[row] = (total * sign * (1.0 - u * u)).astype(BF16).astype(F32)
    for row in range(NB):
        parts = nn(dz_out[row].astype(BF16), by_check[row])
        for slot in range(TPC):
            tile = slot * NB + row
            acc_out[ints[tile]] += parts[:, slot * BLK : (slot + 1) * BLK] * floats[tile]


def first_body(ints, floats, marg, gv, recvc, recvz, fixed, labels, u_ref, signs, by_check,
               by_var, g_out, q_out, dz_out, acc_out, ret_out, sendc, sendz):
    zmask = floats[2 * TILES + 1]
    for block in range(EXT):
        lanes = slice(block * BLK, (block + 1) * BLK)
        if block < NB:
            y, constants = labels[:, lanes], fixed[:, lanes]
        else:
            ref = recvc if block == NB else recvz
            y, constants = ref[2], ref[3]
        prior, r = constants[0:1], constants[1:2]
        ret_out[0:1, lanes] = r
        message = received(gv, block, recvc, recvz, floats)
        level = marg[(SEC - 1) * SH :, lanes]
        f = r * level + (1.0 - r) * (prior + message)
        g = y * jax.nn.sigmoid(f) - (1.0 - y) * jax.nn.sigmoid(-f)
        if block == NB + 1:
            g = g * zmask
        g_out[block] = g
        q_out[block] = (1.0 - r) * g
    backward_rows(ints, floats, SEC - 1, u_ref, signs, by_check, by_var, q_out, dz_out, acc_out)
    send_edges(acc_out, ints, sendc, sendz)


def next_gradient(section, g_in, acc_in, recvc, recvz, th_ref, ret, floats, block):
    r = ret[0:1, block * BLK : (block + 1) * BLK]
    th = th_ref[block, section * SH : (section + 1) * SH, :]
    down = received(acc_in, block, recvc, recvz, floats)
    return r * g_in[block] + 0.5 * down * (1.0 - th * th)


def step_body(section, ints, floats, g_in, acc_in, recvc, recvz, ret, th_ref, u_ref, signs, by_check,
              by_var, g_out, q_out, dz_out, acc_out, sendc, sendz):
    for block in range(EXT):
        g = next_gradient(section + 1, g_in, acc_in, recvc, recvz, th_ref, ret, floats, block)
        g_out[block] = g
        r = ret[0:1, block * BLK : (block + 1) * BLK]
        q_out[block] = (1.0 - r) * g
    backward_rows(ints, floats, section, u_ref, signs, by_check, by_var, q_out, dz_out, acc_out)
    send_edges(acc_out, ints, sendc, sendz)


def weights_body(section_high, count, ints, *refs):
    th_ref, u_ref, by_check, gate_in, msg_in = refs[:5]
    q_refs = refs[5 : 5 + count]
    dz_refs = refs[5 + count : 5 + 2 * count]
    gate_out, msg_out = refs[5 + 2 * count :]
    first = (section_high - count + 1) * SH
    rows = slice(first, first + count * SH)
    for row in range(NB):
        dz = jnp.concatenate([ref[row] for ref in dz_refs], axis=0).astype(BF16)
        gates = nn(dz, by_check[row])
        msgs = nn(u_ref[row, rows, :].astype(BF16), by_check[row])
        for slot in range(TPC):
            tile = slot * NB + row
            lanes = slice(slot * BLK, (slot + 1) * BLK)
            column = ints[tile]
            gate = gates[:, lanes] * th_ref[column, rows, :].astype(BF16).astype(F32)
            gate_out[tile] = gate_in[tile] + jnp.sum(gate.reshape(count, SH, BLK), axis=0)
            q = jnp.concatenate([ref[column] for ref in q_refs], axis=0).astype(BF16).astype(F32)
            msg = msgs[:, lanes] * q
            msg_out[tile] = msg_in[tile] + jnp.sum(msg.reshape(count, SH, BLK), axis=0)


def prepare_body(pattern, by_check, by_var):
    for row in range(PREP_ROWS):
        for slot in range(TPC):
            lanes = slice(slot * BLK, (slot + 1) * BLK)
            tile = pattern[slot, row].astype(F32)
            by_check[row, :, lanes] = tile.astype(BF16)
            by_var[row, lanes, :] = tile.T.astype(BF16)


def prepare(pattern):
    return pl.pallas_call(
        prepare_body,
        grid=(NB // PREP_ROWS,),
        in_specs=[pl.BlockSpec((TPC, PREP_ROWS, BLK, BLK), lambda i: (0, i, 0, 0))],
        out_specs=[
            pl.BlockSpec((PREP_ROWS, BLK, TPC * BLK), lambda i: (i, 0, 0)),
            pl.BlockSpec((PREP_ROWS, TPC * BLK, BLK), lambda i: (i, 0, 0)),
        ],
        out_shape=[
            jax.ShapeDtypeStruct((NB, BLK, TPC * BLK), BF16),
            jax.ShapeDtypeStruct((NB, TPC * BLK, BLK), BF16),
        ],
        compiler_params=pltpu.CompilerParams(vmem_limit_bytes=VMEM_LIMIT),
        cost_estimate=pl.CostEstimate(flops=10**9, bytes_accessed=6 * 2**20, transcendentals=0),
    )(pattern.reshape(TPC, NB, BLK, BLK))


def split(value):
    high = value.astype(BF16).astype(F32)
    return high, value - high


def pack_body(floats, acc_in, recvc, recvz, ret, th_ref, gate, msg, *refs):
    g_refs = refs[:SEC]
    out = refs[SEC]
    for block in range(NB):
        lanes = slice(block * BLK, (block + 1) * BLK)
        entering = [next_gradient(0, g_refs[0], acc_in, recvc, recvz, th_ref, ret, floats, block)]
        entering += [g_refs[section][block] for section in range(SEC - 1)]
        for pair in range(SEC // 2):
            both = jnp.concatenate(entering[2 * pair : 2 * pair + 2], axis=0)
            out[pair * 2 * SH : (pair + 1) * 2 * SH, lanes] = both.astype(BF16)
    priors = []
    for block in range(NB):
        total = g_refs[0][block]
        for section in range(1, SEC):
            total = total + g_refs[section][block]
        r = ret[0:1, block * BLK : (block + 1) * BLK]
        priors.append((1.0 - r) * jnp.sum(total, axis=0, keepdims=True))
    prior_high, prior_low = [], []
    for half in range(2):
        high, low = split(jnp.concatenate(priors[half * SH : (half + 1) * SH], axis=0))
        prior_high.append(high)
        prior_low.append(low)
    gate_rows = jnp.sum(gate[...], axis=1)
    msg_rows = jnp.sum(msg[...], axis=1)
    gate_sum = jnp.sum(gate_rows, axis=1, keepdims=True)
    msg_sum = jnp.sum(msg_rows, axis=1, keepdims=True)
    tile_index = lax.broadcasted_iota(jnp.int32, (TILES, BLK), 0)
    lane_index = lax.broadcasted_iota(jnp.int32, (TILES, BLK), 1)
    rows = []
    for value in (gate_sum, msg_sum):
        placed = jnp.where(tile_index == lane_index, value, 0.0)
        rows += split(jnp.sum(placed, axis=0, keepdims=True))
    weights = jnp.concatenate(rows + [jnp.zeros((SH - 4, BLK), F32)], axis=0)
    for index, value in enumerate(prior_high + prior_low + [weights]):
        doubled = jnp.concatenate([value, value], axis=0).astype(BF16)
        lanes = slice(LANES + index * BLK, LANES + (index + 1) * BLK)
        for pair in range(SEC // 2):
            out[pair * 2 * SH : (pair + 1) * 2 * SH, lanes] = doubled


def unpack_body(got, live, out, gate_out, msg_out, prior_out):
    for block in range(NB):
        lanes = slice(block * BLK, (block + 1) * BLK)
        out[:, lanes] = got[:, lanes].astype(F32)
    grads = []
    for index in range(GRAD_LANES // BLK):
        lanes = slice(LANES + index * BLK, LANES + (index + 1) * BLK)
        grads.append(jnp.sum(got[:, lanes].astype(F32).reshape(SEC, SH, BLK), axis=0))
    prior_out[:SH] = grads[0] + grads[2]
    prior_out[SH:] = grads[1] + grads[3]
    gate_out[...] = (grads[4][0:1] + grads[4][1:2])[:, :TILES] * live[...]
    msg_out[...] = (grads[4][2:3] + grads[4][3:4])[:, :TILES] * live[...]


def on_device(
    checkpoint,
    prior_llr,
    retention,
    syndrome,
    labels,
    tile_cols,
    tile_count,
    pattern,
    gate_weight,
    msg_weight,
):
    shard = lax.axis_index("tile")
    group = lax.axis_index("section")
    even = shard % 2 == 0
    has_z = jnp.logical_and(shard != 0, shard != SEC - 1)

    def own_edges(x):
        first, last = x[..., :BLK], x[..., -BLK:]
        return jnp.where(even, last, first), jnp.where(even, first, last)

    def exchange(core, z):
        return lax.ppermute(core, "tile", CORE_PAIRS), lax.ppermute(z, "tile", Z_PAIRS)

    levels = checkpoint[0]
    my_labels = lax.dynamic_slice_in_dim(labels, group * SH, SH, 0).astype(F32)
    my_signs = 1.0 - 2.0 * lax.dynamic_slice_in_dim(syndrome, group * SH, SH, 0).astype(F32)
    fixed = jnp.concatenate(
        [prior_llr[None], retention[None], jnp.zeros((SH - 2, LANES), F32)], axis=0
    )
    halo_core, halo_z = exchange(*own_edges(levels))

    slots = jnp.arange(TILES, dtype=jnp.int32)
    live = (slots < tile_count[0]).astype(F32)
    low_slot = jnp.where(even, NB + 1, NB)
    high_slot = jnp.where(even, NB, NB + 1)
    columns = jnp.where(
        tile_cols == 0, low_slot, jnp.where(tile_cols == NB + 1, high_slot, tile_cols - 1)
    )
    core_side = jnp.where(even, NB - 1, 0)
    z_side = jnp.where(even, 0, NB - 1)
    ints = jnp.concatenate([columns, core_side[None], z_side[None]]).astype(jnp.int32)
    floats = jnp.concatenate(
        [gate_weight * live, msg_weight * live, jnp.stack([even, has_z]).astype(F32)]
    )
    sent = jnp.concatenate([levels, halo_core, halo_z], axis=1).astype(jnp.float16)
    sent = sent.reshape(SEC, SH, EXT * BLK)
    sent, pattern = lax.optimization_barrier((sent, pattern))
    patterns = prepare(pattern)
    marg = lax.all_to_all(sent, "section", 0, 0, tiled=True)
    marg = marg.reshape(SEC * SH, EXT * BLK).astype(F32)

    def shape(*dims, dtype=F32):
        return jax.ShapeDtypeStruct(dims, dtype)

    edge = shape(2, SH, BLK)
    wide_edge = shape(4, SH, BLK)
    field = shape(EXT, SH, BLK)
    rows = shape(NB, SH, BLK)
    th, u, gv, core, z = call(
        forward_body,
        [shape(EXT, SEC * SH, BLK), shape(NB, SEC * SH, BLK), field, wide_edge, wide_edge],
        [ints, floats, marg, *patterns, my_signs, my_labels, fixed],
        2,
        scratch=[pltpu.VMEM((EXT, SEC * SH, BLK), BF16)],
    )
    core, z = exchange(core, z)
    g, q, dz, acc, ret_ext, core, z = call(
        first_body,
        [field, field, rows, field, shape(1, EXT * BLK), edge, edge],
        [ints, floats, marg, gv, core, z, fixed, my_labels, u, my_signs, *patterns],
        2,
    )
    leaving = {SEC - 1: g}
    saved = [(q, dz)]
    gate = jnp.zeros((TILES, SH, BLK), F32)
    msg = jnp.zeros((TILES, SH, BLK), F32)
    group_size = 4
    for section in reversed(range(SEC - 1)):
        core, z = exchange(core, z)
        if not saved:
            core, z, gate, msg = lax.optimization_barrier((core, z, gate, msg))
        g, q, dz, acc, core, z = call(
            functools.partial(step_body, section),
            [field, field, rows, field, edge, edge],
            [ints, floats, g, acc, core, z, ret_ext, th, u, my_signs, *patterns],
            2,
        )
        leaving[section] = g
        saved.append((q, dz))
        if len(saved) == group_size:
            saved = saved[::-1]
            gate, msg = call(
                functools.partial(weights_body, section + group_size - 1, group_size),
                [shape(TILES, SH, BLK)] * 2,
                [ints, th, u, patterns[0], gate, msg] + [s[0] for s in saved] + [s[1] for s in saved],
                1,
                flops=2 * 2 * group_size * SH * TILES * BLK * BLK,
                bytes_accessed=4 * 2**20,
            )
            saved = []
    core, z = exchange(core, z)
    (packed,) = call(
        pack_body,
        [shape(SEC * SH, LANES + GRAD_LANES, dtype=BF16)],
        [floats, acc, core, z, ret_ext, th, gate, msg] + [leaving[s] for s in range(SEC)],
        1,
    )
    got = lax.all_to_all(packed.reshape(SEC, SH, LANES + GRAD_LANES), "section", 0, 0, tiled=True)
    input_grads, gate, msg, prior = call(
        unpack_body,
        [shape(SEC * SH, LANES), shape(1, TILES), shape(1, TILES), shape(NB, BLK)],
        [got.reshape(SEC * SH, LANES + GRAD_LANES), live[None]],
        0,
    )
    return input_grads[None], gate.reshape(TILES), msg.reshape(TILES), prior.reshape(LANES)


def solution(mesh):
    placed = (
        P("section", None, "tile"),
        P("tile"),
        P("tile"),
        P(None, "tile"),
        P(None, "tile"),
        P("tile"),
        P("tile"),
        P("tile", None, None),
        P("tile"),
        P("tile"),
    )
    return jax.shard_map(
        on_device,
        mesh=mesh,
        in_specs=placed,
        out_specs=(P("section", None, "tile"), P("tile"), P("tile"), P("tile")),
        check_vma=False,
    )
```

```python
import functools

import jax
import jax.numpy as jnp
from jax import lax
from jax.experimental import pallas as pl
from jax.experimental.pallas import tpu as pltpu
from jax.sharding import PartitionSpec as P

BLK = 128
NB = 16
EXT = NB + 2
TPC = 3
TILES = NB * TPC
SEC = 16
SH = 8
GRAD_LANES = 640
LANES = NB * BLK
VMEM_LIMIT = 8 * 1024 * 1024
PREP_ROWS = 4
F32 = jnp.float32
BF16 = jnp.bfloat16
VSPEC = pl.BlockSpec(memory_space=pltpu.VMEM)

CORE_PAIRS = [(i, i ^ 1) for i in range(16)]
Z_PAIRS = [(i, (i + 1) % 16 if i % 2 else (i - 1) % 16) for i in range(16)]


def nn(a, b):
    return lax.dot_general(a, b, (((1,), (0,)), ((), ())), preferred_element_type=F32)


def call(body, outs, args, scratch=(), flops=0, bytes_accessed=0):
    return pl.pallas_call(
        body,
        out_shape=outs,
        in_specs=[VSPEC] * len(args),
        out_specs=[VSPEC] * len(outs),
        scratch_shapes=list(scratch),
        compiler_params=pltpu.CompilerParams(vmem_limit_bytes=VMEM_LIMIT),
        cost_estimate=pl.CostEstimate(flops=flops, bytes_accessed=bytes_accessed, transcendentals=0),
    )(*args)


def scalars(ref):
    return [ref[index, 0] for index in range(TILES + 2)]


class Rows:
    def __init__(self, ref):
        self.ref = ref

    def __getitem__(self, index):
        return self.ref[index : index + 1, :]


def send_edges(acc_ref, ints, sendc, sendz):
    sendc[0] = acc_ref[NB]
    sendc[1] = acc_ref[ints[TILES]]
    sendz[0] = acc_ref[NB + 1]
    sendz[1] = acc_ref[ints[TILES + 1]]


def received(acc_ref, block, recvc, recvz, floats):
    own = acc_ref[block]
    even = floats[2 * TILES]
    zmask = floats[2 * TILES + 1]
    if block == 0:
        return own + (recvz[0] * (zmask * even) + recvc[0] * (1.0 - even))
    if block == NB - 1:
        return own + (recvz[0] * (zmask * (1.0 - even)) + recvc[0] * even)
    if block == NB:
        return own + recvc[1]
    if block == NB + 1:
        return (own + recvz[1]) * zmask
    return own


def forward_body(ints, floats, marg, by_check, by_var, signs, labels, fixed, th_out, u_out, gv_out, sendc, sendz, tb):
    ints, floats = scalars(ints), Rows(floats)
    zmask = floats[2 * TILES + 1]
    for block in range(EXT):
        th = jnp.tanh(0.5 * marg[:, block * BLK : (block + 1) * BLK])
        if block == NB + 1:
            th = th * zmask
        th_out[block] = th
        tb[block] = th.astype(BF16)
    gv_out[...] = jnp.zeros_like(gv_out)
    for row in range(NB):
        total = None
        for slot in range(TPC):
            tile = slot * NB + row
            part = nn(tb[ints[tile]], by_var[row, slot * BLK : (slot + 1) * BLK, :]) * floats[tile]
            total = part if total is None else total + part
        sign = signs[:, row * BLK : (row + 1) * BLK]
        soft = jnp.tanh(total).reshape(SEC, SH, BLK) * sign[None]
        u_out[row] = soft.reshape(SEC * SH, BLK)
    for row in range(NB):
        parts = nn(u_out[row, (SEC - 1) * SH :, :].astype(BF16), by_check[row])
        for slot in range(TPC):
            tile = slot * NB + row
            gv_out[ints[tile]] += parts[:, slot * BLK : (slot + 1) * BLK] * floats[TILES + tile]
    send_edges(gv_out, ints, sendc, sendz)
    even = floats[2 * TILES]
    for source, row in ((labels[...], 2), (fixed[...], 3)):
        first, last = source[:, :BLK], source[:, -BLK:]
        sendc[row] = last * even + first * (1.0 - even)
        sendz[row] = first * even + last * (1.0 - even)


def backward_rows(ints, floats, section, u_ref, signs, by_check, by_var, qs, dz_out, acc_out):
    acc_out[...] = jnp.zeros_like(acc_out)
    for row in range(NB):
        tiles = [slot * NB + row for slot in range(TPC)]
        scaled = [(qs[ints[tile]] * floats[TILES + tile]).astype(BF16) for tile in tiles]
        total = nn(jnp.concatenate(scaled, axis=1), by_var[row])
        u = u_ref[row, section * SH : (section + 1) * SH, :]
        sign = signs[:, row * BLK : (row + 1) * BLK]
        dz_out[row] = (total * sign * (1.0 - u * u)).astype(BF16).astype(F32)
    for row in range(NB):
        parts = nn(dz_out[row].astype(BF16), by_check[row])
        for slot in range(TPC):
            tile = slot * NB + row
            acc_out[ints[tile]] += parts[:, slot * BLK : (slot + 1) * BLK] * floats[tile]


def first_body(ints, floats, marg, gv, recvc, recvz, fixed, labels, u_ref, signs, by_check,
               by_var, g_out, q_out, dz_out, acc_out, ret_out, sendc, sendz):
    ints, floats = scalars(ints), Rows(floats)
    zmask = floats[2 * TILES + 1]
    for block in range(EXT):
        lanes = slice(block * BLK, (block + 1) * BLK)
        if block < NB:
            y, constants = labels[:, lanes], fixed[:, lanes]
        else:
            ref = recvc if block == NB else recvz
            y, constants = ref[2], ref[3]
        prior, r = constants[0:1], constants[1:2]
        ret_out[0:1, lanes] = r
        message = received(gv, block, recvc, recvz, floats)
        level = marg[(SEC - 1) * SH :, lanes]
        f = r * level + (1.0 - r) * (prior + message)
        g = y * jax.nn.sigmoid(f) - (1.0 - y) * jax.nn.sigmoid(-f)
        if block == NB + 1:
            g = g * zmask
        g_out[block] = g
        q_out[block] = (1.0 - r) * g
    backward_rows(ints, floats, SEC - 1, u_ref, signs, by_check, by_var, q_out, dz_out, acc_out)
    send_edges(acc_out, ints, sendc, sendz)


def next_gradient(section, g_in, acc_in, recvc, recvz, th_ref, ret, floats, block):
    r = ret[0:1, block * BLK : (block + 1) * BLK]
    th = th_ref[block, section * SH : (section + 1) * SH, :]
    down = received(acc_in, block, recvc, recvz, floats)
    return r * g_in[block] + 0.5 * down * (1.0 - th * th)


def step_body(section, ints, floats, g_in, acc_in, recvc, recvz, ret, th_ref, u_ref, signs, by_check,
              by_var, g_out, q_out, dz_out, acc_out, sendc, sendz):
    ints, floats = scalars(ints), Rows(floats)
    for block in range(EXT):
        g = next_gradient(section + 1, g_in, acc_in, recvc, recvz, th_ref, ret, floats, block)
        g_out[block] = g
        r = ret[0:1, block * BLK : (block + 1) * BLK]
        q_out[block] = (1.0 - r) * g
    backward_rows(ints, floats, section, u_ref, signs, by_check, by_var, q_out, dz_out, acc_out)
    send_edges(acc_out, ints, sendc, sendz)


def weights_body(section_high, count, ints, *refs):
    ints = scalars(ints)
    th_ref, u_ref, by_check, gate_in, msg_in = refs[:5]
    q_refs = refs[5 : 5 + count]
    dz_refs = refs[5 + count : 5 + 2 * count]
    gate_out, msg_out = refs[5 + 2 * count :]
    first = (section_high - count + 1) * SH
    rows = slice(first, first + count * SH)
    for row in range(NB):
        dz = jnp.concatenate([ref[row] for ref in dz_refs], axis=0).astype(BF16)
        gates = nn(dz, by_check[row])
        msgs = nn(u_ref[row, rows, :].astype(BF16), by_check[row])
        for slot in range(TPC):
            tile = slot * NB + row
            lanes = slice(slot * BLK, (slot + 1) * BLK)
            column = ints[tile]
            gate = gates[:, lanes] * th_ref[column, rows, :].astype(BF16).astype(F32)
            gate_out[tile] = gate_in[tile] + jnp.sum(gate.reshape(count, SH, BLK), axis=0)
            q = jnp.concatenate([ref[column] for ref in q_refs], axis=0).astype(BF16).astype(F32)
            msg = msgs[:, lanes] * q
            msg_out[tile] = msg_in[tile] + jnp.sum(msg.reshape(count, SH, BLK), axis=0)


def prepare_body(pattern, by_check, by_var):
    for row in range(PREP_ROWS):
        for slot in range(TPC):
            lanes = slice(slot * BLK, (slot + 1) * BLK)
            tile = pattern[slot, row].astype(F32)
            by_check[row, :, lanes] = tile.astype(BF16)
            by_var[row, lanes, :] = tile.T.astype(BF16)


def prepare(pattern):
    return pl.pallas_call(
        prepare_body,
        grid=(NB // PREP_ROWS,),
        in_specs=[pl.BlockSpec((TPC, PREP_ROWS, BLK, BLK), lambda i: (0, i, 0, 0))],
        out_specs=[
            pl.BlockSpec((PREP_ROWS, BLK, TPC * BLK), lambda i: (i, 0, 0)),
            pl.BlockSpec((PREP_ROWS, TPC * BLK, BLK), lambda i: (i, 0, 0)),
        ],
        out_shape=[
            jax.ShapeDtypeStruct((NB, BLK, TPC * BLK), BF16),
            jax.ShapeDtypeStruct((NB, TPC * BLK, BLK), BF16),
        ],
        compiler_params=pltpu.CompilerParams(vmem_limit_bytes=VMEM_LIMIT),
        cost_estimate=pl.CostEstimate(flops=10**9, bytes_accessed=6 * 2**20, transcendentals=0),
    )(pattern.reshape(TPC, NB, BLK, BLK))


def split(value):
    high = value.astype(BF16).astype(F32)
    return high, value - high


def pack_body(floats, acc_in, recvc, recvz, ret, th_ref, gate, msg, *refs):
    floats = Rows(floats)
    g_refs = refs[:SEC]
    out = refs[SEC]
    for block in range(NB):
        lanes = slice(block * BLK, (block + 1) * BLK)
        entering = [next_gradient(0, g_refs[0], acc_in, recvc, recvz, th_ref, ret, floats, block)]
        entering += [g_refs[section][block] for section in range(SEC - 1)]
        for pair in range(SEC // 2):
            both = jnp.concatenate(entering[2 * pair : 2 * pair + 2], axis=0)
            out[pair * 2 * SH : (pair + 1) * 2 * SH, lanes] = both.astype(BF16)
    priors = []
    for block in range(NB):
        total = g_refs[0][block]
        for section in range(1, SEC):
            total = total + g_refs[section][block]
        r = ret[0:1, block * BLK : (block + 1) * BLK]
        priors.append((1.0 - r) * jnp.sum(total, axis=0, keepdims=True))
    prior_high, prior_low = [], []
    for half in range(2):
        high, low = split(jnp.concatenate(priors[half * SH : (half + 1) * SH], axis=0))
        prior_high.append(high)
        prior_low.append(low)
    gate_rows = jnp.sum(gate[...], axis=1)
    msg_rows = jnp.sum(msg[...], axis=1)
    gate_sum = jnp.sum(gate_rows, axis=1, keepdims=True)
    msg_sum = jnp.sum(msg_rows, axis=1, keepdims=True)
    tile_index = lax.broadcasted_iota(jnp.int32, (TILES, BLK), 0)
    lane_index = lax.broadcasted_iota(jnp.int32, (TILES, BLK), 1)
    rows = []
    for value in (gate_sum, msg_sum):
        placed = jnp.where(tile_index == lane_index, value, 0.0)
        rows += split(jnp.sum(placed, axis=0, keepdims=True))
    weights = jnp.concatenate(rows + [jnp.zeros((SH - 4, BLK), F32)], axis=0)
    for index, value in enumerate(prior_high + prior_low + [weights]):
        doubled = jnp.concatenate([value, value], axis=0).astype(BF16)
        lanes = slice(LANES + index * BLK, LANES + (index + 1) * BLK)
        for pair in range(SEC // 2):
            out[pair * 2 * SH : (pair + 1) * 2 * SH, lanes] = doubled


def unpack_body(got, live, out, gate_out, msg_out, prior_out):
    for block in range(NB):
        lanes = slice(block * BLK, (block + 1) * BLK)
        out[:, lanes] = got[:, lanes].astype(F32)
    grads = []
    for index in range(GRAD_LANES // BLK):
        lanes = slice(LANES + index * BLK, LANES + (index + 1) * BLK)
        grads.append(jnp.sum(got[:, lanes].astype(F32).reshape(SEC, SH, BLK), axis=0))
    prior_out[:SH] = grads[0] + grads[2]
    prior_out[SH:] = grads[1] + grads[3]
    gate_out[...] = (grads[4][0:1] + grads[4][1:2])[:, :TILES] * live[...]
    msg_out[...] = (grads[4][2:3] + grads[4][3:4])[:, :TILES] * live[...]


def on_device(
    checkpoint,
    prior_llr,
    retention,
    syndrome,
    labels,
    tile_cols,
    tile_count,
    pattern,
    gate_weight,
    msg_weight,
):
    shard = lax.axis_index("tile")
    group = lax.axis_index("section")
    even = shard % 2 == 0
    has_z = jnp.logical_and(shard != 0, shard != SEC - 1)

    def own_edges(x):
        first, last = x[..., :BLK], x[..., -BLK:]
        return jnp.where(even, last, first), jnp.where(even, first, last)

    def exchange(core, z):
        return lax.ppermute(core, "tile", CORE_PAIRS), lax.ppermute(z, "tile", Z_PAIRS)

    levels = checkpoint[0]
    my_labels = lax.dynamic_slice_in_dim(labels, group * SH, SH, 0).astype(F32)
    my_signs = 1.0 - 2.0 * lax.dynamic_slice_in_dim(syndrome, group * SH, SH, 0).astype(F32)
    fixed = jnp.concatenate(
        [prior_llr[None], retention[None], jnp.zeros((SH - 2, LANES), F32)], axis=0
    )
    halo_core, halo_z = exchange(*own_edges(levels))

    slots = jnp.arange(TILES, dtype=jnp.int32)
    live = (slots < tile_count[0]).astype(F32)
    low_slot = jnp.where(even, NB + 1, NB)
    high_slot = jnp.where(even, NB, NB + 1)
    columns = jnp.where(
        tile_cols == 0, low_slot, jnp.where(tile_cols == NB + 1, high_slot, tile_cols - 1)
    )
    core_side = jnp.where(even, NB - 1, 0)
    z_side = jnp.where(even, 0, NB - 1)
    ints = jnp.concatenate([columns, core_side[None], z_side[None]]).astype(jnp.int32)
    ints = jnp.broadcast_to(ints[:, None], (TILES + 2, BLK))
    floats = jnp.concatenate(
        [gate_weight * live, msg_weight * live, jnp.stack([even, has_z]).astype(F32)]
    )
    floats = jnp.broadcast_to(floats[:, None], (2 * TILES + 2, BLK))
    sent = jnp.concatenate([levels, halo_core, halo_z], axis=1).astype(jnp.float16)
    sent = sent.reshape(SEC, SH, EXT * BLK)
    sent, pattern = lax.optimization_barrier((sent, pattern))
    patterns = prepare(pattern)
    marg = lax.all_to_all(sent, "section", 0, 0, tiled=True)
    marg = marg.reshape(SEC * SH, EXT * BLK).astype(F32)

    def shape(*dims, dtype=F32):
        return jax.ShapeDtypeStruct(dims, dtype)

    edge = shape(2, SH, BLK)
    wide_edge = shape(4, SH, BLK)
    field = shape(EXT, SH, BLK)
    rows = shape(NB, SH, BLK)
    th, u, gv, core, z = call(
        forward_body,
        [shape(EXT, SEC * SH, BLK), shape(NB, SEC * SH, BLK), field, wide_edge, wide_edge],
        [ints, floats, marg, *patterns, my_signs, my_labels, fixed],
        scratch=[pltpu.VMEM((EXT, SEC * SH, BLK), BF16)],
    )
    core, z = exchange(core, z)
    g, q, dz, acc, ret_ext, core, z = call(
        first_body,
        [field, field, rows, field, shape(1, EXT * BLK), edge, edge],
        [ints, floats, marg, gv, core, z, fixed, my_labels, u, my_signs, *patterns],
    )
    leaving = {SEC - 1: g}
    saved = [(q, dz)]
    gate = jnp.zeros((TILES, SH, BLK), F32)
    msg = jnp.zeros((TILES, SH, BLK), F32)
    group_size = 4
    for section in reversed(range(SEC - 1)):
        core, z = exchange(core, z)
        if not saved:
            core, z, gate, msg = lax.optimization_barrier((core, z, gate, msg))
        g, q, dz, acc, core, z = call(
            functools.partial(step_body, section),
            [field, field, rows, field, edge, edge],
            [ints, floats, g, acc, core, z, ret_ext, th, u, my_signs, *patterns],
        )
        leaving[section] = g
        saved.append((q, dz))
        if len(saved) == group_size:
            saved = saved[::-1]
            gate, msg = call(
                functools.partial(weights_body, section + group_size - 1, group_size),
                [shape(TILES, SH, BLK)] * 2,
                [ints, th, u, patterns[0], gate, msg] + [s[0] for s in saved] + [s[1] for s in saved],
                flops=2 * 2 * group_size * SH * TILES * BLK * BLK,
                bytes_accessed=4 * 2**20,
            )
            saved = []
    core, z = exchange(core, z)
    (packed,) = call(
        pack_body,
        [shape(SEC * SH, LANES + GRAD_LANES, dtype=BF16)],
        [floats, acc, core, z, ret_ext, th, gate, msg] + [leaving[s] for s in range(SEC)],
    )
    got = lax.all_to_all(packed.reshape(SEC, SH, LANES + GRAD_LANES), "section", 0, 0, tiled=True)
    input_grads, gate, msg, prior = call(
        unpack_body,
        [shape(SEC * SH, LANES), shape(1, TILES), shape(1, TILES), shape(NB, BLK)],
        [got.reshape(SEC * SH, LANES + GRAD_LANES), live[None]],
    )
    return input_grads[None], gate.reshape(TILES), msg.reshape(TILES), prior.reshape(LANES)


def solution(mesh):
    placed = (
        P("section", None, "tile"),
        P("tile"),
        P("tile"),
        P(None, "tile"),
        P(None, "tile"),
        P("tile"),
        P("tile"),
        P("tile", None, None),
        P("tile"),
        P("tile"),
    )
    return jax.shard_map(
        on_device,
        mesh=mesh,
        in_specs=placed,
        out_specs=(P("section", None, "tile"), P("tile"), P("tile"), P("tile")),
        check_vma=False,
    )
```

```python
import functools

import jax
import jax.numpy as jnp
from jax import lax
from jax.experimental import pallas as pl
from jax.experimental.pallas import tpu as pltpu
from jax.sharding import PartitionSpec as P

BLK = 128
NB = 16
EXT = NB + 2
TPC = 3
TILES = NB * TPC
SEC = 16
SH = 8
GRAD_LANES = 640
LANES = NB * BLK
VMEM_LIMIT = 8 * 1024 * 1024
PREP_ROWS = 4
F32 = jnp.float32
BF16 = jnp.bfloat16
VSPEC = pl.BlockSpec(memory_space=pltpu.VMEM)

CORE_PAIRS = [(i, i ^ 1) for i in range(16)]
Z_PAIRS = [(i, (i + 1) % 16 if i % 2 else (i - 1) % 16) for i in range(16)]


def nn(a, b):
    return lax.dot_general(a, b, (((1,), (0,)), ((), ())), preferred_element_type=F32)


def call(body, outs, args, scratch=(), flops=0, bytes_accessed=0):
    return pl.pallas_call(
        body,
        out_shape=outs,
        in_specs=[VSPEC] * len(args),
        out_specs=[VSPEC] * len(outs),
        scratch_shapes=list(scratch),
        compiler_params=pltpu.CompilerParams(vmem_limit_bytes=VMEM_LIMIT),
        cost_estimate=pl.CostEstimate(flops=flops, bytes_accessed=bytes_accessed, transcendentals=0),
    )(*args)


def scalars(ref):
    return [ref[index, 0] for index in range(TILES + 2)]


class Rows:
    def __init__(self, ref):
        self.ref = ref

    def __getitem__(self, index):
        return self.ref[index : index + 1, :]


def send_edges(acc_ref, ints, sendc, sendz):
    sendc[0] = acc_ref[NB]
    sendc[1] = acc_ref[ints[TILES]]
    sendz[0] = acc_ref[NB + 1]
    sendz[1] = acc_ref[ints[TILES + 1]]


def received(acc_ref, block, recvc, recvz, floats):
    own = acc_ref[block]
    even = floats[2 * TILES]
    zmask = floats[2 * TILES + 1]
    if block == 0:
        return own + (recvz[0] * (zmask * even) + recvc[0] * (1.0 - even))
    if block == NB - 1:
        return own + (recvz[0] * (zmask * (1.0 - even)) + recvc[0] * even)
    if block == NB:
        return own + recvc[1]
    if block == NB + 1:
        return (own + recvz[1]) * zmask
    return own


def forward_body(ints, floats, marg, by_var, signs, th_out, u_out, tb):
    ints, floats = scalars(ints), Rows(floats)
    zmask = floats[2 * TILES + 1]
    for block in range(EXT):
        th = jnp.tanh(0.5 * marg[:, block * BLK : (block + 1) * BLK])
        if block == NB + 1:
            th = th * zmask
        th_out[block] = th
        tb[block] = th.astype(BF16)
    for row in range(NB):
        total = None
        for slot in range(TPC):
            tile = slot * NB + row
            part = nn(tb[ints[tile]], by_var[row, slot * BLK : (slot + 1) * BLK, :]) * floats[tile]
            total = part if total is None else total + part
        sign = signs[:, row * BLK : (row + 1) * BLK]
        soft = jnp.tanh(total).reshape(SEC, SH, BLK) * sign[None]
        u_out[row] = soft.reshape(SEC * SH, BLK)


def message_body(ints, floats, marg, by_check, by_var, signs, labels, fixed, gv_out, sendc, sendz, th, us):
    ints, floats = scalars(ints), Rows(floats)
    zmask = floats[2 * TILES + 1]
    for block in range(EXT):
        value = jnp.tanh(0.5 * marg[:, block * BLK : (block + 1) * BLK])
        if block == NB + 1:
            value = value * zmask
        th[block] = value
    gv_out[...] = jnp.zeros_like(gv_out)
    for row in range(NB):
        total = None
        for slot in range(TPC):
            tile = slot * NB + row
            chosen = th[ints[tile]].astype(BF16)
            part = nn(chosen, by_var[row, slot * BLK : (slot + 1) * BLK, :]) * floats[tile]
            total = part if total is None else total + part
        us[row] = jnp.tanh(total) * signs[:, row * BLK : (row + 1) * BLK]
    for row in range(NB):
        parts = nn(us[row].astype(BF16), by_check[row])
        for slot in range(TPC):
            tile = slot * NB + row
            gv_out[ints[tile]] += parts[:, slot * BLK : (slot + 1) * BLK] * floats[TILES + tile]
    send_edges(gv_out, ints, sendc, sendz)
    even = floats[2 * TILES]
    for source, row in ((labels[...], 2), (fixed[...], 3)):
        first, last = source[:, :BLK], source[:, -BLK:]
        sendc[row] = last * even + first * (1.0 - even)
        sendz[row] = first * even + last * (1.0 - even)


def backward_rows(ints, floats, section, u_ref, signs, by_check, by_var, qs, dz_out, acc_out):
    acc_out[...] = jnp.zeros_like(acc_out)
    for row in range(NB):
        tiles = [slot * NB + row for slot in range(TPC)]
        scaled = [(qs[ints[tile]] * floats[TILES + tile]).astype(BF16) for tile in tiles]
        total = nn(jnp.concatenate(scaled, axis=1), by_var[row])
        u = u_ref[row, section * SH : (section + 1) * SH, :]
        sign = signs[:, row * BLK : (row + 1) * BLK]
        dz_out[row] = (total * sign * (1.0 - u * u)).astype(BF16).astype(F32)
    for row in range(NB):
        parts = nn(dz_out[row].astype(BF16), by_check[row])
        for slot in range(TPC):
            tile = slot * NB + row
            acc_out[ints[tile]] += parts[:, slot * BLK : (slot + 1) * BLK] * floats[tile]


def first_body(ints, floats, marg, gv, recvc, recvz, fixed, labels, u_ref, signs, by_check,
               by_var, g_out, q_out, dz_out, acc_out, ret_out, sendc, sendz):
    ints, floats = scalars(ints), Rows(floats)
    zmask = floats[2 * TILES + 1]
    for block in range(EXT):
        lanes = slice(block * BLK, (block + 1) * BLK)
        if block < NB:
            y, constants = labels[:, lanes], fixed[:, lanes]
        else:
            ref = recvc if block == NB else recvz
            y, constants = ref[2], ref[3]
        prior, r = constants[0:1], constants[1:2]
        ret_out[0:1, lanes] = r
        message = received(gv, block, recvc, recvz, floats)
        level = marg[:, lanes]
        f = r * level + (1.0 - r) * (prior + message)
        g = y * jax.nn.sigmoid(f) - (1.0 - y) * jax.nn.sigmoid(-f)
        if block == NB + 1:
            g = g * zmask
        g_out[block] = g
        q_out[block] = (1.0 - r) * g
    backward_rows(ints, floats, SEC - 1, u_ref, signs, by_check, by_var, q_out, dz_out, acc_out)
    send_edges(acc_out, ints, sendc, sendz)


def next_gradient(section, g_in, acc_in, recvc, recvz, th_ref, ret, floats, block):
    r = ret[0:1, block * BLK : (block + 1) * BLK]
    th = th_ref[block, section * SH : (section + 1) * SH, :]
    down = received(acc_in, block, recvc, recvz, floats)
    return r * g_in[block] + 0.5 * down * (1.0 - th * th)


def step_body(section, ints, floats, g_in, acc_in, recvc, recvz, ret, th_ref, u_ref, signs, by_check,
              by_var, g_out, q_out, dz_out, acc_out, sendc, sendz):
    ints, floats = scalars(ints), Rows(floats)
    for block in range(EXT):
        g = next_gradient(section + 1, g_in, acc_in, recvc, recvz, th_ref, ret, floats, block)
        g_out[block] = g
        r = ret[0:1, block * BLK : (block + 1) * BLK]
        q_out[block] = (1.0 - r) * g
    backward_rows(ints, floats, section, u_ref, signs, by_check, by_var, q_out, dz_out, acc_out)
    send_edges(acc_out, ints, sendc, sendz)


def weights_body(section_high, count, ints, *refs):
    ints = scalars(ints)
    th_ref, u_ref, by_check, gate_in, msg_in = refs[:5]
    q_refs = refs[5 : 5 + count]
    dz_refs = refs[5 + count : 5 + 2 * count]
    gate_out, msg_out = refs[5 + 2 * count :]
    first = (section_high - count + 1) * SH
    rows = slice(first, first + count * SH)
    for row in range(NB):
        dz = jnp.concatenate([ref[row] for ref in dz_refs], axis=0).astype(BF16)
        gates = nn(dz, by_check[row])
        msgs = nn(u_ref[row, rows, :].astype(BF16), by_check[row])
        for slot in range(TPC):
            tile = slot * NB + row
            lanes = slice(slot * BLK, (slot + 1) * BLK)
            column = ints[tile]
            gate = gates[:, lanes] * th_ref[column, rows, :].astype(BF16).astype(F32)
            gate_out[tile] = gate_in[tile] + jnp.sum(gate.reshape(count, SH, BLK), axis=0)
            q = jnp.concatenate([ref[column] for ref in q_refs], axis=0).astype(BF16).astype(F32)
            msg = msgs[:, lanes] * q
            msg_out[tile] = msg_in[tile] + jnp.sum(msg.reshape(count, SH, BLK), axis=0)


def prepare_body(pattern, by_check, by_var):
    for row in range(PREP_ROWS):
        for slot in range(TPC):
            lanes = slice(slot * BLK, (slot + 1) * BLK)
            tile = pattern[slot, row].astype(F32)
            by_check[row, :, lanes] = tile.astype(BF16)
            by_var[row, lanes, :] = tile.T.astype(BF16)


def prepare(pattern):
    return pl.pallas_call(
        prepare_body,
        grid=(NB // PREP_ROWS,),
        in_specs=[pl.BlockSpec((TPC, PREP_ROWS, BLK, BLK), lambda i: (0, i, 0, 0))],
        out_specs=[
            pl.BlockSpec((PREP_ROWS, BLK, TPC * BLK), lambda i: (i, 0, 0)),
            pl.BlockSpec((PREP_ROWS, TPC * BLK, BLK), lambda i: (i, 0, 0)),
        ],
        out_shape=[
            jax.ShapeDtypeStruct((NB, BLK, TPC * BLK), BF16),
            jax.ShapeDtypeStruct((NB, TPC * BLK, BLK), BF16),
        ],
        compiler_params=pltpu.CompilerParams(vmem_limit_bytes=VMEM_LIMIT),
        cost_estimate=pl.CostEstimate(flops=10**9, bytes_accessed=6 * 2**20, transcendentals=0),
    )(pattern.reshape(TPC, NB, BLK, BLK))


def split(value):
    high = value.astype(BF16).astype(F32)
    return high, value - high


def pack_body(floats, acc_in, recvc, recvz, ret, th_ref, gate, msg, *refs):
    floats = Rows(floats)
    g_refs = refs[:SEC]
    out = refs[SEC]
    for block in range(NB):
        lanes = slice(block * BLK, (block + 1) * BLK)
        entering = [next_gradient(0, g_refs[0], acc_in, recvc, recvz, th_ref, ret, floats, block)]
        entering += [g_refs[section][block] for section in range(SEC - 1)]
        for pair in range(SEC // 2):
            both = jnp.concatenate(entering[2 * pair : 2 * pair + 2], axis=0)
            out[pair * 2 * SH : (pair + 1) * 2 * SH, lanes] = both.astype(BF16)
    priors = []
    for block in range(NB):
        total = g_refs[0][block]
        for section in range(1, SEC):
            total = total + g_refs[section][block]
        r = ret[0:1, block * BLK : (block + 1) * BLK]
        priors.append((1.0 - r) * jnp.sum(total, axis=0, keepdims=True))
    prior_high, prior_low = [], []
    for half in range(2):
        high, low = split(jnp.concatenate(priors[half * SH : (half + 1) * SH], axis=0))
        prior_high.append(high)
        prior_low.append(low)
    gate_rows = jnp.sum(gate[...], axis=1)
    msg_rows = jnp.sum(msg[...], axis=1)
    gate_sum = jnp.sum(gate_rows, axis=1, keepdims=True)
    msg_sum = jnp.sum(msg_rows, axis=1, keepdims=True)
    tile_index = lax.broadcasted_iota(jnp.int32, (TILES, BLK), 0)
    lane_index = lax.broadcasted_iota(jnp.int32, (TILES, BLK), 1)
    rows = []
    for value in (gate_sum, msg_sum):
        placed = jnp.where(tile_index == lane_index, value, 0.0)
        rows += split(jnp.sum(placed, axis=0, keepdims=True))
    weights = jnp.concatenate(rows + [jnp.zeros((SH - 4, BLK), F32)], axis=0)
    for index, value in enumerate(prior_high + prior_low + [weights]):
        doubled = jnp.concatenate([value, value], axis=0).astype(BF16)
        lanes = slice(LANES + index * BLK, LANES + (index + 1) * BLK)
        for pair in range(SEC // 2):
            out[pair * 2 * SH : (pair + 1) * 2 * SH, lanes] = doubled


def unpack_body(got, live, out, gate_out, msg_out, prior_out):
    for block in range(NB):
        lanes = slice(block * BLK, (block + 1) * BLK)
        out[:, lanes] = got[:, lanes].astype(F32)
    grads = []
    for index in range(GRAD_LANES // BLK):
        lanes = slice(LANES + index * BLK, LANES + (index + 1) * BLK)
        grads.append(jnp.sum(got[:, lanes].astype(F32).reshape(SEC, SH, BLK), axis=0))
    prior_out[:SH] = grads[0] + grads[2]
    prior_out[SH:] = grads[1] + grads[3]
    gate_out[...] = (grads[4][0:1] + grads[4][1:2])[:, :TILES] * live[...]
    msg_out[...] = (grads[4][2:3] + grads[4][3:4])[:, :TILES] * live[...]


def on_device(
    checkpoint,
    prior_llr,
    retention,
    syndrome,
    labels,
    tile_cols,
    tile_count,
    pattern,
    gate_weight,
    msg_weight,
):
    shard = lax.axis_index("tile")
    group = lax.axis_index("section")
    even = shard % 2 == 0
    has_z = jnp.logical_and(shard != 0, shard != SEC - 1)

    def own_edges(x):
        first, last = x[..., :BLK], x[..., -BLK:]
        return jnp.where(even, last, first), jnp.where(even, first, last)

    def exchange(core, z):
        return lax.ppermute(core, "tile", CORE_PAIRS), lax.ppermute(z, "tile", Z_PAIRS)

    levels = checkpoint[0]
    fixed = jnp.concatenate(
        [prior_llr[None], retention[None], jnp.zeros((SH - 2, LANES), F32)], axis=0
    )
    halo_core, halo_z = exchange(*own_edges(levels))

    slots = jnp.arange(TILES, dtype=jnp.int32)
    live = (slots < tile_count[0]).astype(F32)
    low_slot = jnp.where(even, NB + 1, NB)
    high_slot = jnp.where(even, NB, NB + 1)
    columns = jnp.where(
        tile_cols == 0, low_slot, jnp.where(tile_cols == NB + 1, high_slot, tile_cols - 1)
    )
    core_side = jnp.where(even, NB - 1, 0)
    z_side = jnp.where(even, 0, NB - 1)
    ints = jnp.concatenate([columns, core_side[None], z_side[None]]).astype(jnp.int32)
    ints = jnp.broadcast_to(ints[:, None], (TILES + 2, BLK))
    floats = jnp.concatenate(
        [gate_weight * live, msg_weight * live, jnp.stack([even, has_z]).astype(F32)]
    )
    floats = jnp.broadcast_to(floats[:, None], (2 * TILES + 2, BLK))
    sent = jnp.concatenate([levels, halo_core, halo_z], axis=1).astype(jnp.float16)
    sent = sent.reshape(SEC, SH, EXT * BLK)
    sent, pattern, labels, syndrome = lax.optimization_barrier((sent, pattern, labels, syndrome))
    my_labels = lax.dynamic_slice_in_dim(labels, group * SH, SH, 0).astype(F32)
    my_signs = 1.0 - 2.0 * lax.dynamic_slice_in_dim(syndrome, group * SH, SH, 0).astype(F32)
    patterns = prepare(pattern)
    marg = lax.all_to_all(sent, "section", 0, 0, tiled=True)
    last_marg = marg[SEC - 1].astype(F32)

    def shape(*dims, dtype=F32):
        return jax.ShapeDtypeStruct(dims, dtype)

    edge = shape(2, SH, BLK)
    wide_edge = shape(4, SH, BLK)
    field = shape(EXT, SH, BLK)
    rows = shape(NB, SH, BLK)
    gv, core, z = call(
        message_body,
        [field, wide_edge, wide_edge],
        [ints, floats, last_marg, *patterns, my_signs, my_labels, fixed],
        scratch=[pltpu.VMEM((EXT, SH, BLK), F32), pltpu.VMEM((NB, SH, BLK), F32)],
    )
    core, z, marg = lax.optimization_barrier((core, z, marg))
    th, u = call(
        forward_body,
        [shape(EXT, SEC * SH, BLK), shape(NB, SEC * SH, BLK)],
        [ints, floats, marg.reshape(SEC * SH, EXT * BLK).astype(F32), patterns[1], my_signs],
        scratch=[pltpu.VMEM((EXT, SEC * SH, BLK), BF16)],
        flops=2 * SEC * SH * TILES * BLK * BLK,
        bytes_accessed=4 * 2**20,
    )
    core, z = exchange(core, z)
    g, q, dz, acc, ret_ext, core, z = call(
        first_body,
        [field, field, rows, field, shape(1, EXT * BLK), edge, edge],
        [ints, floats, last_marg, gv, core, z, fixed, my_labels, u, my_signs, *patterns],
    )
    leaving = {SEC - 1: g}
    saved = [(q, dz)]
    gate = jnp.zeros((TILES, SH, BLK), F32)
    msg = jnp.zeros((TILES, SH, BLK), F32)
    group_size = 4
    for section in reversed(range(SEC - 1)):
        core, z = exchange(core, z)
        if not saved:
            core, z, gate, msg = lax.optimization_barrier((core, z, gate, msg))
        g, q, dz, acc, core, z = call(
            functools.partial(step_body, section),
            [field, field, rows, field, edge, edge],
            [ints, floats, g, acc, core, z, ret_ext, th, u, my_signs, *patterns],
        )
        leaving[section] = g
        saved.append((q, dz))
        if len(saved) == group_size:
            saved = saved[::-1]
            gate, msg = call(
                functools.partial(weights_body, section + group_size - 1, group_size),
                [shape(TILES, SH, BLK)] * 2,
                [ints, th, u, patterns[0], gate, msg] + [s[0] for s in saved] + [s[1] for s in saved],
                flops=2 * 2 * group_size * SH * TILES * BLK * BLK,
                bytes_accessed=4 * 2**20,
            )
            saved = []
    core, z = exchange(core, z)
    (packed,) = call(
        pack_body,
        [shape(SEC * SH, LANES + GRAD_LANES, dtype=BF16)],
        [floats, acc, core, z, ret_ext, th, gate, msg] + [leaving[s] for s in range(SEC)],
    )
    got = lax.all_to_all(packed.reshape(SEC, SH, LANES + GRAD_LANES), "section", 0, 0, tiled=True)
    input_grads, gate, msg, prior = call(
        unpack_body,
        [shape(SEC * SH, LANES), shape(1, TILES), shape(1, TILES), shape(NB, BLK)],
        [got.reshape(SEC * SH, LANES + GRAD_LANES), live[None]],
    )
    return input_grads[None], gate.reshape(TILES), msg.reshape(TILES), prior.reshape(LANES)


def solution(mesh):
    placed = (
        P("section", None, "tile"),
        P("tile"),
        P("tile"),
        P(None, "tile"),
        P(None, "tile"),
        P("tile"),
        P("tile"),
        P("tile", None, None),
        P("tile"),
        P("tile"),
    )
    return jax.shard_map(
        on_device,
        mesh=mesh,
        in_specs=placed,
        out_specs=(P("section", None, "tile"), P("tile"), P("tile"), P("tile")),
        check_vma=False,
    )
```

```python
import functools

import jax
import jax.numpy as jnp
from jax import lax
from jax.experimental import pallas as pl
from jax.experimental.pallas import tpu as pltpu
from jax.sharding import PartitionSpec as P

BLK = 128
NB = 16
EXT = NB + 2
TPC = 3
TILES = NB * TPC
SEC = 16
SH = 8
GRAD_LANES = 640
LANES = NB * BLK
VMEM_LIMIT = 8 * 1024 * 1024
PREP_ROWS = 4
F32 = jnp.float32
BF16 = jnp.bfloat16
VSPEC = pl.BlockSpec(memory_space=pltpu.VMEM)

CORE_PAIRS = [(i, i ^ 1) for i in range(16)]
Z_PAIRS = [(i, (i + 1) % 16 if i % 2 else (i - 1) % 16) for i in range(16)]


def nn(a, b):
    return lax.dot_general(a, b, (((1,), (0,)), ((), ())), preferred_element_type=F32)


def call(body, outs, args, scratch=(), flops=0, bytes_accessed=0):
    return pl.pallas_call(
        body,
        out_shape=outs,
        in_specs=[VSPEC] * len(args),
        out_specs=[VSPEC] * len(outs),
        scratch_shapes=list(scratch),
        compiler_params=pltpu.CompilerParams(vmem_limit_bytes=VMEM_LIMIT),
        cost_estimate=pl.CostEstimate(flops=flops, bytes_accessed=bytes_accessed, transcendentals=0),
    )(*args)


def scalars(ref):
    return [ref[index, 0] for index in range(TILES + 2)]


class Rows:
    def __init__(self, ref):
        self.ref = ref

    def __getitem__(self, index):
        return self.ref[index : index + 1, :]


def send_edges(acc_ref, ints, sendc, sendz):
    sendc[0] = acc_ref[NB]
    sendc[1] = acc_ref[ints[TILES]]
    sendz[0] = acc_ref[NB + 1]
    sendz[1] = acc_ref[ints[TILES + 1]]


def received(acc_ref, block, recvc, recvz, floats):
    own = acc_ref[block]
    even = floats[2 * TILES]
    zmask = floats[2 * TILES + 1]
    if block == 0:
        return own + (recvz[0] * (zmask * even) + recvc[0] * (1.0 - even))
    if block == NB - 1:
        return own + (recvz[0] * (zmask * (1.0 - even)) + recvc[0] * even)
    if block == NB:
        return own + recvc[1]
    if block == NB + 1:
        return (own + recvz[1]) * zmask
    return own


def forward_body(ints, floats, marg, by_var, signs, th_out, u_out, tb):
    ints, floats = scalars(ints), Rows(floats)
    zmask = floats[2 * TILES + 1]
    for block in range(EXT):
        th = jnp.tanh(0.5 * marg[:, block * BLK : (block + 1) * BLK])
        if block == NB + 1:
            th = th * zmask
        th_out[block] = th
        tb[block] = th.astype(BF16)
    for row in range(NB):
        total = None
        for slot in range(TPC):
            tile = slot * NB + row
            part = nn(tb[ints[tile]], by_var[row, slot * BLK : (slot + 1) * BLK, :]) * floats[tile]
            total = part if total is None else total + part
        sign = signs[:, row * BLK : (row + 1) * BLK]
        soft = jnp.tanh(total).reshape(SEC, SH, BLK) * sign[None]
        u_out[row] = soft.reshape(SEC * SH, BLK)


def message_body(ints, floats, marg, by_check, by_var, signs, labels, fixed, gv_out, sendc, sendz, th, us):
    ints, floats = scalars(ints), Rows(floats)
    zmask = floats[2 * TILES + 1]
    for block in range(EXT):
        value = jnp.tanh(0.5 * marg[:, block * BLK : (block + 1) * BLK])
        if block == NB + 1:
            value = value * zmask
        th[block] = value
    gv_out[...] = jnp.zeros_like(gv_out)
    for row in range(NB):
        total = None
        for slot in range(TPC):
            tile = slot * NB + row
            chosen = th[ints[tile]].astype(BF16)
            part = nn(chosen, by_var[row, slot * BLK : (slot + 1) * BLK, :]) * floats[tile]
            total = part if total is None else total + part
        us[row] = jnp.tanh(total) * signs[:, row * BLK : (row + 1) * BLK]
    for row in range(NB):
        parts = nn(us[row].astype(BF16), by_check[row])
        for slot in range(TPC):
            tile = slot * NB + row
            gv_out[ints[tile]] += parts[:, slot * BLK : (slot + 1) * BLK] * floats[TILES + tile]
    send_edges(gv_out, ints, sendc, sendz)
    even = floats[2 * TILES]
    for source, row in ((labels[...], 2), (fixed[...], 3)):
        first, last = source[:, :BLK], source[:, -BLK:]
        sendc[row] = last * even + first * (1.0 - even)
        sendz[row] = first * even + last * (1.0 - even)


def backward_rows(ints, floats, section, u_ref, signs, by_check, by_var, qs, dz_out, acc_out):
    acc_out[...] = jnp.zeros_like(acc_out)
    for row in range(NB):
        tiles = [slot * NB + row for slot in range(TPC)]
        scaled = [(qs[ints[tile]] * floats[TILES + tile]).astype(BF16) for tile in tiles]
        total = nn(jnp.concatenate(scaled, axis=1), by_var[row])
        u = u_ref[row, section * SH : (section + 1) * SH, :]
        sign = signs[:, row * BLK : (row + 1) * BLK]
        dz_out[row] = (total * sign * (1.0 - u * u)).astype(BF16).astype(F32)
    for row in range(NB):
        parts = nn(dz_out[row].astype(BF16), by_check[row])
        for slot in range(TPC):
            tile = slot * NB + row
            acc_out[ints[tile]] += parts[:, slot * BLK : (slot + 1) * BLK] * floats[tile]


def first_body(ints, floats, marg, gv, recvc, recvz, fixed, labels, u_ref, signs, by_check,
               by_var, g_out, q_out, dz_out, acc_out, ret_out, sendc, sendz):
    ints, floats = scalars(ints), Rows(floats)
    zmask = floats[2 * TILES + 1]
    for block in range(EXT):
        lanes = slice(block * BLK, (block + 1) * BLK)
        if block < NB:
            y, constants = labels[:, lanes], fixed[:, lanes]
        else:
            ref = recvc if block == NB else recvz
            y, constants = ref[2], ref[3]
        prior, r = constants[0:1], constants[1:2]
        ret_out[0:1, lanes] = r
        message = received(gv, block, recvc, recvz, floats)
        level = marg[:, lanes]
        f = r * level + (1.0 - r) * (prior + message)
        g = y * jax.nn.sigmoid(f) - (1.0 - y) * jax.nn.sigmoid(-f)
        if block == NB + 1:
            g = g * zmask
        g_out[block] = g
        q_out[block] = (1.0 - r) * g
    backward_rows(ints, floats, SEC - 1, u_ref, signs, by_check, by_var, q_out, dz_out, acc_out)
    send_edges(acc_out, ints, sendc, sendz)


def next_gradient(section, g_in, acc_in, recvc, recvz, th_ref, ret, floats, block):
    r = ret[0:1, block * BLK : (block + 1) * BLK]
    th = th_ref[block, section * SH : (section + 1) * SH, :]
    down = received(acc_in, block, recvc, recvz, floats)
    return r * g_in[block] + 0.5 * down * (1.0 - th * th)


def step_body(section, ints, floats, g_in, acc_in, recvc, recvz, ret, th_ref, u_ref, signs, by_check,
              by_var, g_out, q_out, dz_out, acc_out, sendc, sendz):
    ints, floats = scalars(ints), Rows(floats)
    for block in range(EXT):
        g = next_gradient(section + 1, g_in, acc_in, recvc, recvz, th_ref, ret, floats, block)
        g_out[block] = g
        r = ret[0:1, block * BLK : (block + 1) * BLK]
        q_out[block] = (1.0 - r) * g
    backward_rows(ints, floats, section, u_ref, signs, by_check, by_var, q_out, dz_out, acc_out)
    send_edges(acc_out, ints, sendc, sendz)


def weights_body(section_high, count, ints, *refs):
    ints = scalars(ints)
    th_ref, u_ref, by_check, gate_in, msg_in = refs[:5]
    q_refs = refs[5 : 5 + count]
    dz_refs = refs[5 + count : 5 + 2 * count]
    gate_out, msg_out = refs[5 + 2 * count :]
    first = (section_high - count + 1) * SH
    rows = slice(first, first + count * SH)
    for row in range(NB):
        dz = jnp.concatenate([ref[row] for ref in dz_refs], axis=0).astype(BF16)
        gates = nn(dz, by_check[row])
        msgs = nn(u_ref[row, rows, :].astype(BF16), by_check[row])
        for slot in range(TPC):
            tile = slot * NB + row
            lanes = slice(slot * BLK, (slot + 1) * BLK)
            column = ints[tile]
            gate = gates[:, lanes] * th_ref[column, rows, :].astype(BF16).astype(F32)
            gate_out[tile] = gate_in[tile] + jnp.sum(gate.reshape(count, SH, BLK), axis=0)
            q = jnp.concatenate([ref[column] for ref in q_refs], axis=0).astype(BF16).astype(F32)
            msg = msgs[:, lanes] * q
            msg_out[tile] = msg_in[tile] + jnp.sum(msg.reshape(count, SH, BLK), axis=0)


def prepare_body(pattern, by_check, by_var):
    for row in range(PREP_ROWS):
        for slot in range(TPC):
            lanes = slice(slot * BLK, (slot + 1) * BLK)
            tile = pattern[slot, row].astype(F32)
            by_check[row, :, lanes] = tile.astype(BF16)
            by_var[row, lanes, :] = tile.T.astype(BF16)


def prepare(pattern):
    return pl.pallas_call(
        prepare_body,
        grid=(NB // PREP_ROWS,),
        in_specs=[pl.BlockSpec((TPC, PREP_ROWS, BLK, BLK), lambda i: (0, i, 0, 0))],
        out_specs=[
            pl.BlockSpec((PREP_ROWS, BLK, TPC * BLK), lambda i: (i, 0, 0)),
            pl.BlockSpec((PREP_ROWS, TPC * BLK, BLK), lambda i: (i, 0, 0)),
        ],
        out_shape=[
            jax.ShapeDtypeStruct((NB, BLK, TPC * BLK), BF16),
            jax.ShapeDtypeStruct((NB, TPC * BLK, BLK), BF16),
        ],
        compiler_params=pltpu.CompilerParams(vmem_limit_bytes=VMEM_LIMIT),
        cost_estimate=pl.CostEstimate(flops=10**9, bytes_accessed=6 * 2**20, transcendentals=0),
    )(pattern.reshape(TPC, NB, BLK, BLK))


def split(value):
    high = value.astype(BF16).astype(F32)
    return high, value - high


def pack_body(floats, acc_in, recvc, recvz, ret, th_ref, gate, msg, *refs):
    floats = Rows(floats)
    g_refs = refs[:SEC]
    out = refs[SEC]
    for block in range(NB):
        lanes = slice(block * BLK, (block + 1) * BLK)
        entering = [next_gradient(0, g_refs[0], acc_in, recvc, recvz, th_ref, ret, floats, block)]
        entering += [g_refs[section][block] for section in range(SEC - 1)]
        for pair in range(SEC // 2):
            both = jnp.concatenate(entering[2 * pair : 2 * pair + 2], axis=0)
            out[pair * 2 * SH : (pair + 1) * 2 * SH, lanes] = both.astype(BF16)
    priors = []
    for block in range(NB):
        total = g_refs[0][block]
        for section in range(1, SEC):
            total = total + g_refs[section][block]
        r = ret[0:1, block * BLK : (block + 1) * BLK]
        priors.append((1.0 - r) * jnp.sum(total, axis=0, keepdims=True))
    prior_high, prior_low = [], []
    for half in range(2):
        high, low = split(jnp.concatenate(priors[half * SH : (half + 1) * SH], axis=0))
        prior_high.append(high)
        prior_low.append(low)
    gate_rows = jnp.sum(gate[...], axis=1)
    msg_rows = jnp.sum(msg[...], axis=1)
    gate_sum = jnp.sum(gate_rows, axis=1, keepdims=True)
    msg_sum = jnp.sum(msg_rows, axis=1, keepdims=True)
    tile_index = lax.broadcasted_iota(jnp.int32, (TILES, BLK), 0)
    lane_index = lax.broadcasted_iota(jnp.int32, (TILES, BLK), 1)
    rows = []
    for value in (gate_sum, msg_sum):
        placed = jnp.where(tile_index == lane_index, value, 0.0)
        rows += split(jnp.sum(placed, axis=0, keepdims=True))
    weights = jnp.concatenate(rows + [jnp.zeros((SH - 4, BLK), F32)], axis=0)
    for index, value in enumerate(prior_high + prior_low + [weights]):
        doubled = jnp.concatenate([value, value], axis=0).astype(BF16)
        lanes = slice(LANES + index * BLK, LANES + (index + 1) * BLK)
        for pair in range(SEC // 2):
            out[pair * 2 * SH : (pair + 1) * 2 * SH, lanes] = doubled


def unpack_body(got, live, out, gate_out, msg_out, prior_out):
    for block in range(NB):
        lanes = slice(block * BLK, (block + 1) * BLK)
        out[:, lanes] = got[:, lanes].astype(F32)
    grads = []
    for index in range(GRAD_LANES // BLK):
        lanes = slice(LANES + index * BLK, LANES + (index + 1) * BLK)
        grads.append(jnp.sum(got[:, lanes].astype(F32).reshape(SEC, SH, BLK), axis=0))
    prior_out[:SH] = grads[0] + grads[2]
    prior_out[SH:] = grads[1] + grads[3]
    gate_out[...] = (grads[4][0:1] + grads[4][1:2])[:, :TILES] * live[...]
    msg_out[...] = (grads[4][2:3] + grads[4][3:4])[:, :TILES] * live[...]


def on_device(
    checkpoint,
    prior_llr,
    retention,
    syndrome,
    labels,
    tile_cols,
    tile_count,
    pattern,
    gate_weight,
    msg_weight,
):
    shard = lax.axis_index("tile")
    group = lax.axis_index("section")
    even = shard % 2 == 0
    has_z = jnp.logical_and(shard != 0, shard != SEC - 1)

    def own_edges(x):
        first, last = x[..., :BLK], x[..., -BLK:]
        return jnp.where(even, last, first), jnp.where(even, first, last)

    def exchange(core, z):
        return lax.ppermute(core, "tile", CORE_PAIRS), lax.ppermute(z, "tile", Z_PAIRS)

    levels = lax.optimization_barrier(checkpoint[0].astype(jnp.float16))
    fixed = jnp.concatenate(
        [prior_llr[None], retention[None], jnp.zeros((SH - 2, LANES), F32)], axis=0
    )
    halo_core, halo_z = exchange(*own_edges(levels))

    slots = jnp.arange(TILES, dtype=jnp.int32)
    live = (slots < tile_count[0]).astype(F32)
    low_slot = jnp.where(even, NB + 1, NB)
    high_slot = jnp.where(even, NB, NB + 1)
    columns = jnp.where(
        tile_cols == 0, low_slot, jnp.where(tile_cols == NB + 1, high_slot, tile_cols - 1)
    )
    core_side = jnp.where(even, NB - 1, 0)
    z_side = jnp.where(even, 0, NB - 1)
    ints = jnp.concatenate([columns, core_side[None], z_side[None]]).astype(jnp.int32)
    ints = jnp.broadcast_to(ints[:, None], (TILES + 2, BLK))
    floats = jnp.concatenate(
        [gate_weight * live, msg_weight * live, jnp.stack([even, has_z]).astype(F32)]
    )
    floats = jnp.broadcast_to(floats[:, None], (2 * TILES + 2, BLK))
    sent = jnp.concatenate([levels, halo_core, halo_z], axis=1)
    sent = sent.reshape(SEC, SH, EXT * BLK)
    sent, pattern, labels, syndrome = lax.optimization_barrier((sent, pattern, labels, syndrome))
    my_labels = lax.dynamic_slice_in_dim(labels, group * SH, SH, 0).astype(F32)
    my_signs = 1.0 - 2.0 * lax.dynamic_slice_in_dim(syndrome, group * SH, SH, 0).astype(F32)
    patterns = prepare(pattern)
    marg = lax.all_to_all(sent, "section", 0, 0, tiled=True)
    last_marg = marg[SEC - 1].astype(F32)

    def shape(*dims, dtype=F32):
        return jax.ShapeDtypeStruct(dims, dtype)

    edge = shape(2, SH, BLK)
    wide_edge = shape(4, SH, BLK)
    field = shape(EXT, SH, BLK)
    rows = shape(NB, SH, BLK)
    gv, core, z = call(
        message_body,
        [field, wide_edge, wide_edge],
        [ints, floats, last_marg, *patterns, my_signs, my_labels, fixed],
        scratch=[pltpu.VMEM((EXT, SH, BLK), F32), pltpu.VMEM((NB, SH, BLK), F32)],
    )
    core, z, marg = lax.optimization_barrier((core, z, marg))
    th, u = call(
        forward_body,
        [shape(EXT, SEC * SH, BLK), shape(NB, SEC * SH, BLK)],
        [ints, floats, marg.reshape(SEC * SH, EXT * BLK).astype(F32), patterns[1], my_signs],
        scratch=[pltpu.VMEM((EXT, SEC * SH, BLK), BF16)],
        flops=2 * SEC * SH * TILES * BLK * BLK,
        bytes_accessed=4 * 2**20,
    )
    core, z = exchange(core, z)
    g, q, dz, acc, ret_ext, core, z = call(
        first_body,
        [field, field, rows, field, shape(1, EXT * BLK), edge, edge],
        [ints, floats, last_marg, gv, core, z, fixed, my_labels, u, my_signs, *patterns],
    )
    leaving = {SEC - 1: g}
    saved = [(q, dz)]
    gate = jnp.zeros((TILES, SH, BLK), F32)
    msg = jnp.zeros((TILES, SH, BLK), F32)
    group_size = 4
    for section in reversed(range(SEC - 1)):
        core, z = exchange(core, z)
        if not saved:
            core, z, gate, msg = lax.optimization_barrier((core, z, gate, msg))
        g, q, dz, acc, core, z = call(
            functools.partial(step_body, section),
            [field, field, rows, field, edge, edge],
            [ints, floats, g, acc, core, z, ret_ext, th, u, my_signs, *patterns],
        )
        leaving[section] = g
        saved.append((q, dz))
        if len(saved) == group_size:
            saved = saved[::-1]
            gate, msg = call(
                functools.partial(weights_body, section + group_size - 1, group_size),
                [shape(TILES, SH, BLK)] * 2,
                [ints, th, u, patterns[0], gate, msg] + [s[0] for s in saved] + [s[1] for s in saved],
                flops=2 * 2 * group_size * SH * TILES * BLK * BLK,
                bytes_accessed=4 * 2**20,
            )
            saved = []
    core, z = exchange(core, z)
    (packed,) = call(
        pack_body,
        [shape(SEC * SH, LANES + GRAD_LANES, dtype=BF16)],
        [floats, acc, core, z, ret_ext, th, gate, msg] + [leaving[s] for s in range(SEC)],
    )
    got = lax.all_to_all(packed.reshape(SEC, SH, LANES + GRAD_LANES), "section", 0, 0, tiled=True)
    input_grads, gate, msg, prior = call(
        unpack_body,
        [shape(SEC * SH, LANES), shape(1, TILES), shape(1, TILES), shape(NB, BLK)],
        [got.reshape(SEC * SH, LANES + GRAD_LANES), live[None]],
    )
    return input_grads[None], gate.reshape(TILES), msg.reshape(TILES), prior.reshape(LANES)


def solution(mesh):
    placed = (
        P("section", None, "tile"),
        P("tile"),
        P("tile"),
        P(None, "tile"),
        P(None, "tile"),
        P("tile"),
        P("tile"),
        P("tile", None, None),
        P("tile"),
        P("tile"),
    )
    return jax.shard_map(
        on_device,
        mesh=mesh,
        in_specs=placed,
        out_specs=(P("section", None, "tile"), P("tile"), P("tile"), P("tile")),
        check_vma=False,
    )
```
